256 devices in a mesh: dp: 8 (over y, core), seq: 4 (over z_lo), tensor: 8 (over x, z_hi).
Axes of the slice: x: 4, y: 4, z: 8 (z_hi: 2, z_lo: 4; z = z_hi * 4 + z_lo), core: 2. Of those that a mesh axis runs over, the one named last changes fastest.
Arguments:
- queries: bfloat16 [8, 1024, 64, 128], P('dp', 'seq', 'tensor'), may hold values from -100 to 100
- keys: bfloat16 [8, 1024, 8, 128], P('dp', 'seq', 'tensor'), may hold values from -5 to 5
- values: bfloat16 [8, 1024, 8, 128], P('dp', 'seq', 'tensor'), may hold values from -6 to 6
- segment_ids: int32 [8, 1024], P('dp', 'seq'), may hold values from 0 to 7, never falling along the last dimension, each value on 1 to 512 neighbouring positions
- codes: int32 [4096, 8192], P(('dp', 'seq'), 'tensor'), may hold values from 0 to 15
- zero_points: int32 [4096, 64], P(('dp', 'seq'), 'tensor'), may hold values from 4 to 11
- step_sizes: bfloat16 [4096, 64], P(('dp', 'seq'), 'tensor'), may hold values from 0.0009994507 to 0.0039978027
- cotangent: bfloat16 [8, 1024, 4096], P('dp', 'seq'), may hold values from -6 to 6
Outputs:
- grad_steps: float32 [4096, 64], P(('dp', 'seq'), 'tensor')
- grad_queries: bfloat16 [8, 1024, 64, 128], P('dp', 'seq', 'tensor')
- key_gradient: bfloat16 [8, 1024, 8, 128], P('dp', 'seq', 'tensor')
- value_gradient: bfloat16 [8, 1024, 8, 128], P('dp', 'seq', 'tensor')
The draws below stay inside these ranges and needn't reach their ends.
Inputs may be any that keep to these rules, and one draw needn't show every extreme that they name: `segment_ids`: documents are runs of consecutive positions numbered from 0 upward.
All inputs are finite; a program needn't handle non-finite values.
Results may differ from the reference program's by a relative error of at most 0.035.
Values may be sent and summed in bfloat16 or wider, within the bound.
A program may use at most 128 MiB of HBM per device.

```python
import math
import jax
import jax.numpy as jnp
import numpy as np
from jax import lax

DOUT = 4096
QUERY_HEADS = 64
KEY_VALUE_HEADS = 8
HEAD_DIMENSION = 128
GROUP = 128
DOCS = 8
SEQUENCE_LENGTH = 1024
PACKED_SEQUENCES = 8
TOKENS = 8192
DOC_MOST = 512


def shared_keys(key):
    return jax.random.truncated_normal(key, -4.5, 4.5, (PACKED_SEQUENCES, SEQUENCE_LENGTH, KEY_VALUE_HEADS, HEAD_DIMENSION), jnp.float32)


def draw_keys(key, part):
    base_offset = shared_keys(key)
    return base_offset.astype(jnp.bfloat16)


def draw_queries(key, part):
    key = jax.random.fold_in(key, 23)
    first = jax.random.fold_in(key, 0)
    fresh = jax.random.truncated_normal(first, -5.0, 5.0, (PACKED_SEQUENCES, SEQUENCE_LENGTH, QUERY_HEADS, HEAD_DIMENSION), jnp.float32)
    return fresh.astype(jnp.bfloat16)


def set_ends(values, rng, low, top_value):
    shape = values.shape
    index_at = [jax.random.randint(jax.random.fold_in(rng, axis), (), 0, shape[axis]) for axis in range(len(shape))]
    values = values.at[tuple(index_at)].set(low)
    longest = shape.index(max(shape))
    index_at[longest] = (index_at[longest] + 1) % shape[longest]
    return values.at[tuple(index_at)].set(top_value)


def steps_of(own_key, shape, cuts, smallest, top_value):
    def one(axis_at, parts):
        draws = jax.random.uniform(jax.random.fold_in(jax.random.fold_in(own_key, 6), axis_at), (parts,), jnp.float32, smallest / len(cuts), top_value / len(cuts))
        return jnp.repeat(jnp.exp(draws), shape[axis_at] // parts).reshape((-1,) + (1,) * (len(shape) - axis_at - 1))

    factor_of = one(*cuts[0])
    for cut in cuts[1:]:
        factor_of = factor_of * one(*cut)
    return factor_of


def length_profile(amount, total, most, slope):
    portions = [(1 << 20) // math.isqrt(rank ** slope) + 1 for rank in range(2, amount + 1)]
    spare, given = total - most - (amount - 1), [1] * (amount - 1)
    while spare > 0:
        candidates = [i for i in range(amount - 1) if given[i] < most]
        whole, remaining = sum([portions[i] for i in candidates]), spare
        for i in candidates:
            more = min(most - given[i], max(1, remaining * portions[i] // whole), spare)
            given[i] = given[i] + more
            spare = spare - more
    return np.array([most] + given)


def uneven(key, number_of, total, limit, lean):
    if number_of == 2:
        one = jax.random.randint(key, (), max(1, total - limit), min(limit, total - 1) + 1)
        return jnp.stack([one, total - one])
    lengths = jnp.asarray(length_profile(number_of, total, limit, lean), jnp.int32)
    couples = (number_of - 1) // 2
    giver, receiver = lengths[1:1 + 2 * couples:2], lengths[2:2 + 2 * couples:2]
    margin = jnp.minimum(giver - 1, limit - receiver)
    moved = jax.random.randint(jax.random.fold_in(key, 1), (couples,), 0, 1 << 20) % (margin + 1)
    lengths = lengths.at[1:1 + 2 * couples:2].set(giver - moved).at[2:2 + 2 * couples:2].set(receiver + moved)
    return lengths[jax.random.permutation(jax.random.fold_in(key, 2), number_of)]


def bell_draw(stream_key, shape, width, reach, cuts=(), kind=jnp.bfloat16):
    result = jax.random.normal(stream_key, shape, jnp.float32) * width
    if len(cuts) > 0:
        result = steps_of(stream_key, shape, cuts, -0.22, 0.18) * result
    return jnp.clip(result, min=-reach, max=reach).astype(kind)


def setup_inputs(seed: int = 0) -> dict:
    seeds = jax.random.split(jax.random.key(seed), 9)
    queries = draw_queries(jax.random.fold_in(seeds[8], 71), 0)
    keys = draw_keys(jax.random.fold_in(seeds[8], 71), 0)
    values = bell_draw(seeds[2], (PACKED_SEQUENCES, SEQUENCE_LENGTH, KEY_VALUE_HEADS, HEAD_DIMENSION), 1.0, 6.0, ((0, 8), (1, 4), (2, 8)))
    segment_ids = jax.vmap(lambda own: jnp.searchsorted(jnp.cumsum(uneven(own, DOCS, SEQUENCE_LENGTH, DOC_MOST, 2)), jnp.arange(SEQUENCE_LENGTH), side="right"))(jax.random.split(seeds[3], PACKED_SEQUENCES)).reshape((PACKED_SEQUENCES, SEQUENCE_LENGTH)).astype(jnp.int32)
    codes = set_ends(jax.random.randint(seeds[4], (DOUT, QUERY_HEADS * HEAD_DIMENSION), 0, 16), jax.random.fold_in(seeds[4], 1), 0, 15).astype(jnp.int32)
    zero_points = set_ends(jax.random.randint(seeds[5], (DOUT, QUERY_HEADS * HEAD_DIMENSION // GROUP), 4, 12), jax.random.fold_in(seeds[5], 1), 4, 11).astype(jnp.int32)
    step_sizes = jnp.clip(jnp.exp(math.log(0.0039978027) - 1.3862944 * jax.random.uniform(seeds[6], (DOUT, QUERY_HEADS * HEAD_DIMENSION // GROUP), jnp.float32) ** steps_of(seeds[6], (DOUT, QUERY_HEADS * HEAD_DIMENSION // GROUP), ((0, 32), (1, 8)), -0.2, 0.2)), 0.0009994507, 0.0039978027).astype(jnp.bfloat16)
    cotangent = bell_draw(seeds[7], (PACKED_SEQUENCES, SEQUENCE_LENGTH, DOUT), 1.0, 6.0, ((0, 8), (1, 4)))
    return {"queries": queries, "keys": keys, "values": values, "segment_ids": segment_ids, "codes": codes, "zero_points": zero_points, "step_sizes": step_sizes, "cotangent": cotangent}


def one_sequence(query_seq, key_seq, value_seq, seg_seq, cot_seq, weight):
    length_count = query_seq.shape[0]
    group_index = QUERY_HEADS // KEY_VALUE_HEADS
    scale_factor = HEAD_DIMENSION ** -0.5
    query_float = query_seq.astype(jnp.float32)
    key_rep = jnp.repeat(key_seq.astype(jnp.float32), group_index, axis=1)
    value_rep = jnp.repeat(value_seq.astype(jnp.float32), group_index, axis=1)
    scores = jnp.einsum('qhd,khd->hqk', query_float, key_rep) * scale_factor
    position = jnp.arange(length_count, dtype=jnp.int32)
    allowed = (position[None, :] <= position[:, None]) & (seg_seq[None, :] == seg_seq[:, None])
    allowed = allowed[None]
    capped = jnp.where(allowed, scores, jnp.float32(-1e30))
    top = jnp.max(capped, axis=-1, keepdims=True)
    expo = jnp.where(allowed, jnp.exp(capped - top), jnp.float32(0.0))
    prob = expo / jnp.sum(expo, axis=-1, keepdims=True)
    attended = jnp.einsum('hqk,khd->qhd', prob, value_rep).astype(jnp.bfloat16)
    flat = attended.reshape(length_count, QUERY_HEADS * HEAD_DIMENSION)
    grad_out = jnp.dot(cot_seq, weight, preferred_element_type=jnp.float32).astype(jnp.bfloat16)
    gradient_float = grad_out.reshape(length_count, QUERY_HEADS, HEAD_DIMENSION).astype(jnp.float32)
    delta = jnp.sum(gradient_float * attended.astype(jnp.float32), axis=-1).T
    probability_lower = lax.optimization_barrier(prob.astype(jnp.bfloat16)).astype(jnp.float32)
    value_gradient = jnp.einsum('vwj,wvi->jvi', probability_lower, gradient_float).reshape(length_count, KEY_VALUE_HEADS, group_index, HEAD_DIMENSION).sum(2)
    grad_prob = jnp.einsum('qhd,khd->hqk', gradient_float, value_rep)
    score_gradient = lax.optimization_barrier((prob * (grad_prob - delta[:, :, None])).astype(jnp.bfloat16)).astype(jnp.float32)
    grad_queries = (jnp.einsum('hqk,khd->qhd', score_gradient, key_rep) * scale_factor).astype(jnp.bfloat16)
    key_gradient = jnp.einsum('vwj,wvi->jvi', score_gradient, query_float).reshape(length_count, KEY_VALUE_HEADS, group_index, HEAD_DIMENSION).sum(2) * scale_factor
    partial_weight = lax.dot_general(cot_seq, flat, (((0,), (0,)), ((), ())), preferred_element_type=jnp.float32)
    return grad_queries, key_gradient.astype(jnp.bfloat16), value_gradient.astype(jnp.bfloat16), partial_weight


def reference(queries, keys, values, segment_ids, codes, zero_points, step_sizes, cotangent):
    centered = (codes - jnp.repeat(zero_points, GROUP, axis=1)).astype(jnp.float32)
    weight = (centered * jnp.repeat(step_sizes.astype(jnp.float32), GROUP, axis=1)).astype(jnp.bfloat16)

    def visit(total, pieces):
        query_seq, key_seq, value_seq, seg_seq, cot_seq = pieces
        grad_q, grad_k, grad_v, partial_weight = one_sequence(query_seq, key_seq, value_seq, seg_seq, cot_seq, weight)
        return total + partial_weight, (grad_q, grad_k, grad_v)

    start = jnp.zeros((DOUT, QUERY_HEADS * HEAD_DIMENSION), jnp.float32)
    grad_weight, stacked = lax.scan(visit, start, (queries, keys, values, segment_ids, cotangent))
    grad_queries, key_gradient, value_gradient = stacked
    grad_steps = (grad_weight * centered).reshape(DOUT, QUERY_HEADS * HEAD_DIMENSION // GROUP, GROUP).sum(-1) * (TOKENS ** -0.5)
    return grad_steps, grad_queries, key_gradient, value_gradient
```

```python
import jax
import jax.numpy as jnp
from jax import lax
from jax.sharding import PartitionSpec as P

GROUP = 128


def local(queries, keys, values, segment_ids, codes, zero_points, step_sizes, cotangent):
    query_loc = queries[0]
    tok_rows = query_loc.shape[0]
    heads_loc = query_loc.shape[1]
    head_size = query_loc.shape[2]
    kv_heads = keys.shape[2]
    group_index = heads_loc // kv_heads
    features = heads_loc * head_size
    groups_loc = features // GROUP
    scale_factor = head_size ** (-0.5)
    seg_low = segment_ids.astype(jnp.bfloat16)
    whole_keys, whole_values, whole_seg = (
        lax.all_gather(keys, "seq", axis=1, tiled=True),
        lax.all_gather(values, "seq", axis=1, tiled=True),
        lax.all_gather(seg_low, "seq", axis=1, tiled=True),
    )
    key_all = whole_keys[0]
    value_all = whole_values[0]
    seg_all = whole_seg[0]
    length_count = key_all.shape[0]
    query_grp = query_loc.reshape(tok_rows, kv_heads, group_index, head_size)
    scores = (
        jnp.einsum("qcgd,kcd->cgqk", query_grp, key_all, preferred_element_type=jnp.float32)
        * scale_factor
    )
    query_pos = lax.axis_index("seq") * tok_rows + jnp.arange(tok_rows, dtype=jnp.int32)
    key_pos = jnp.arange(length_count, dtype=jnp.int32)
    allowed = (key_pos[None, :] <= query_pos[:, None]) & (seg_all[None, :] == seg_low[0][:, None])
    allowed = allowed[None, None]
    capped = jnp.where(allowed, scores, jnp.float32(-1e30))
    top = jnp.max(capped, axis=-1, keepdims=True)
    expo = jnp.where(allowed, jnp.exp(capped - top), jnp.float32(0.0))
    prob = expo / jnp.sum(expo, axis=-1, keepdims=True)
    attended = jnp.einsum("cgqk,kcd->qcgd", prob, value_all.astype(jnp.float32)).astype(
        jnp.bfloat16
    )
    flat = attended.reshape(tok_rows, features)
    upstream = cotangent[0]
    centered = codes - jnp.repeat(zero_points, GROUP, axis=1)
    rows_loc = codes.shape[0]
    total_tokens = lax.axis_size("dp") * lax.axis_size("seq") * tok_rows
    weight_loc = (
        centered.astype(jnp.float32) * jnp.repeat(step_sizes.astype(jnp.float32), GROUP, axis=1)
    ).astype(jnp.bfloat16)
    columns = upstream
    weight_all = lax.all_gather(weight_loc, ("dp", "seq"), axis=0, tiled=True)
    grad_acc = jnp.dot(columns, weight_all, preferred_element_type=jnp.float32)
    grad_weight = lax.dot_general(
        columns, flat, (((0,), (0,)), ((), ())), preferred_element_type=jnp.float32
    )
    partial_steps = (
        (grad_weight * weight_all.astype(jnp.float32)).reshape(-1, groups_loc, GROUP).sum(-1)
    )
    summed = lax.psum_scatter(partial_steps, ("dp", "seq"), scatter_dimension=0, tiled=True)
    grad_steps = summed * total_tokens ** (-0.5) / step_sizes.astype(jnp.float32)
    grad_out = grad_acc.astype(jnp.bfloat16).reshape(tok_rows, kv_heads, group_index, head_size)
    delta = jnp.sum(grad_out.astype(jnp.float32) * attended.astype(jnp.float32), axis=-1)
    delta = jnp.transpose(delta, (1, 2, 0))
    probability_lower = prob.astype(jnp.bfloat16)
    grad_prob = jnp.einsum(
        "qcgd,kcd->cgqk", grad_out, value_all, preferred_element_type=jnp.float32
    )
    score_gradient = (prob * (grad_prob - delta[..., None])).astype(jnp.bfloat16)
    grad_query = (
        jnp.einsum("cgqk,kcd->qcgd", score_gradient, key_all, preferred_element_type=jnp.float32)
        * scale_factor
    )
    grad_queries = grad_query.astype(jnp.bfloat16).reshape(1, tok_rows, heads_loc, head_size)
    key_part = (
        jnp.einsum("cgqk,qcgd->kcd", score_gradient, query_grp, preferred_element_type=jnp.float32)
        * scale_factor
    )
    value_part = jnp.einsum(
        "cgqk,qcgd->kcd", probability_lower, grad_out, preferred_element_type=jnp.float32
    )
    key_value = lax.psum_scatter(
        jnp.concatenate([key_part, value_part], axis=-1), "seq", scatter_dimension=0, tiled=True
    )
    key_gradient = key_value[:, :, :head_size].astype(jnp.bfloat16)[None]
    value_gradient = key_value[:, :, head_size:].astype(jnp.bfloat16)[None]
    return (grad_steps, grad_queries, key_gradient, value_gradient)


def solution(mesh):
    in_specs = (
        P("dp", "seq", "tensor", None),
        P("dp", "seq", "tensor", None),
        P("dp", "seq", "tensor", None),
        P("dp", "seq"),
        P(("dp", "seq"), "tensor"),
        P(("dp", "seq"), "tensor"),
        P(("dp", "seq"), "tensor"),
        P("dp", "seq", None),
    )
    out_specs = (
        P(("dp", "seq"), "tensor"),
        P("dp", "seq", "tensor", None),
        P("dp", "seq", "tensor", None),
        P("dp", "seq", "tensor", None),
    )
    return jax.shard_map(local, mesh=mesh, in_specs=in_specs, out_specs=out_specs, check_vma=False)
```

```python
import jax
import jax.numpy as jnp
from jax import lax
from jax.experimental import pallas as pl
from jax.experimental.pallas import tpu as pltpu
from jax.sharding import PartitionSpec as P

MESH = pl.DeviceIdType.MESH
HEADS = 8
HEAD = 128
TOK = 256
DOUT = 4096
BLOCKS = 3
AHEAD = 2
SCALE = HEAD**-0.5
LOG2E = 1.4426950408889634
STEP_SCALE = 8192**-0.5
NT = (((1,), (1,)), ((), ()))


def mm(a, b):
    return jnp.dot(a, b, preferred_element_type=jnp.float32)


def kernel(
    q_hbm, k_ref, v_ref, seg_ref, codes_hbm, zero_ref, step_ref, cot_hbm,
    gs_ref, dq_ref, dk_ref, dv_ref,
    q_in, q_f32, codes, cot, cot_t, wbuf, kv, kv_t, seg, bias, qh, xbuf, ebuf, att, rinv, pacc, dkv,
    p1, r1, p2, r2, r3, dsend, drecv,
    in_sem, zs, zr, zf, ys, yr, fs, fr, ps, pr, kvs, kvr, sgs, sgr, s1, t1, s2, t2, s3, t3, gs_s, gs_r,
):
    dp = lax.axis_index("dp")
    s = lax.axis_index("seq")
    core = lax.rem(dp, 2)
    y = dp // 2
    partner = dp + 1 - 2 * core
    yp = lax.rem(y + 1, 4) * 2 + core
    ym = lax.rem(y + 3, 4) * 2 + core
    y2 = lax.rem(y + 2, 4) * 2 + core

    in_codes = pltpu.make_async_copy(codes_hbm, codes, in_sem.at[0])
    in_q = pltpu.make_async_copy(q_hbm, q_in, in_sem.at[1])
    in_cot = pltpu.make_async_copy(cot_hbm, cot, in_sem.at[2])
    in_codes.start()
    in_q.start()
    in_cot.start()

    barrier = pltpu.get_barrier_semaphore()
    for other in (partner, yp, ym, y2):
        pl.semaphore_signal(barrier, inc=1, device_id={"dp": other}, device_id_type=MESH)
    for k in (1, 2, 3):
        pl.semaphore_signal(
            barrier, inc=1, device_id={"seq": lax.rem(s + k, 4)}, device_id_type=MESH
        )

    def rows(block):
        return pl.ds(pl.multiple_of(block * 128, 128), 128)

    def remote(src, dst, send, recv, **to):
        return pltpu.make_async_remote_copy(
            src, dst, send, recv, device_id=to, device_id_type=MESH
        )

    def zcopy(c, block, to, send):
        part = wbuf.at[c, dp, :, rows(block)]
        return remote(part, part, send, zr.at[c, block], seq=to)

    def ycopy(c, k):
        part = wbuf.at[c, dp]
        return remote(part, part, ys.at[c, k], yr.at[c, k], dp=(yp, ym)[k])

    def fcopy(c, k):
        part = wbuf.at[c, (ym, yp)[k], pl.ds(k * 64, 64)]
        return remote(part, part, fs.at[c, k], fr.at[c, k], dp=(yp, ym)[k])

    def pcopy(c, k):
        part = wbuf.at[c, (dp, ym, yp, y2)[k]]
        return remote(part, part, ps.at[c, k], pr.at[c, k], dp=partner)

    def near(to):
        return (jnp.abs(s - to) == 1) | (jnp.abs(s - to) == 2)

    def z_start(c):
        for to in range(4):
            @pl.when(near(to))
            def _():
                zcopy(c, s, to, zs.at[c, to]).start()

    def z_arrive(c):
        @pl.when(s == 2)
        def _():
            zcopy(c, 0, 0, zf.at[c]).wait_recv()
            zcopy(c, 0, 3, zf.at[c]).start()

        @pl.when(s == 1)
        def _():
            zcopy(c, 3, 3, zf.at[c]).wait_recv()
            zcopy(c, 3, 0, zf.at[c]).start()

        for block in range(4):
            known = s == block
            if block == 0:
                known = known | (s == 2)
            if block == 3:
                known = known | (s == 1)

            @pl.when(jnp.logical_not(known))
            def _():
                zcopy(c, block, block, zf.at[c]).wait_recv()

    def make_weight(h):
        part = jnp.transpose(codes[:, h * HEAD : (h + 1) * HEAD].astype(jnp.float32))
        zero = zero_ref[h : h + 1, :].astype(jnp.float32)
        step = step_ref[...].astype(jnp.float32)[h : h + 1, :]
        wbuf[h, dp, :, rows(s)] = ((part - zero) * step).astype(jnp.bfloat16)

    def kv_copy(k):
        return remote(kv.at[2], kv.at[1 - k], kvs.at[k], kvr.at[k], seq=s + 1 + k)

    def seg_copy(k):
        return remote(seg.at[2], seg.at[1 - k], sgs.at[k], sgr.at[k], seq=s + 1 + k)

    in_codes.wait()
    make_weight(0)
    make_weight(1)
    pl.semaphore_wait(barrier, 7)
    z_start(0)
    z_start(1)
    kv[2, 0] = k_ref[...]
    kv[2, 1] = v_ref[...]
    seg[2] = jnp.broadcast_to(seg_ref[...], (8, TOK))
    for k in range(2):
        @pl.when(s + 1 + k < 4)
        def _():
            seg_copy(k).start()
            kv_copy(k).start()

        @pl.when(s - 1 - k < 0)
        def _():
            kv[1 - k] = jnp.zeros((2, TOK, HEAD), jnp.bfloat16)
            seg[1 - k] = jnp.full((8, TOK), -1, jnp.int32)

    for h in range(2, HEADS):
        make_weight(h)
    in_q.wait()
    q_f32[...] = q_in[...].astype(jnp.float32).reshape(TOK * HEADS, HEAD)
    for h in range(HEADS):
        qh[h] = q_f32[pl.ds(h, TOK, stride=HEADS), :].astype(jnp.bfloat16)
    in_cot.wait()

    def turn(i, _):
        part = cot[:, pl.ds(pl.multiple_of(i * 512, 512), 512)].astype(jnp.float32)
        cot_t[pl.ds(pl.multiple_of(i * 512, 512), 512), :] = jnp.transpose(part).astype(
            jnp.bfloat16
        )
        return 0

    lax.fori_loop(0, 8, turn, 0)
    dkv[...] = jnp.zeros((2, BLOCKS * TOK, HEAD), jnp.float32)

    def attention_inputs():
        for k in range(2):
            @pl.when(s - 1 - k >= 0)
            def _():
                remote(
                    kv.at[2], kv.at[1 - k], kvs.at[k], kvr.at[k], seq=s - 1 - k
                ).wait_recv()
                remote(
                    seg.at[2], seg.at[1 - k], sgs.at[k], sgr.at[k], seq=s - 1 - k
                ).wait_recv()

        own = seg_ref[...].astype(jnp.float32)
        for j in range(BLOCKS):
            kv_t[0, :, j * TOK : (j + 1) * TOK] = jnp.transpose(
                kv[j, 0].astype(jnp.float32)
            ).astype(jnp.bfloat16)
            kv_t[1, :, j * TOK : (j + 1) * TOK] = jnp.transpose(
                kv[j, 1].astype(jnp.float32)
            ).astype(jnp.bfloat16)
            for half in range(2):
                row = seg[j, 0:1, half * 128 : (half + 1) * 128].astype(jnp.float32)
                column = jnp.transpose(jnp.broadcast_to(row, (128, 128)))
                column = jnp.concatenate([column, column], axis=1)
                allowed = column == own
                if j == BLOCKS - 1:
                    key_pos = half * 128 + lax.broadcasted_iota(jnp.int32, (128, TOK), 0)
                    query_pos = lax.broadcasted_iota(jnp.int32, (128, TOK), 1)
                    allowed = allowed & (key_pos <= query_pos)
                bias[j * TOK + half * 128 : j * TOK + (half + 1) * 128, :] = jnp.where(
                    allowed, jnp.float32(0.0), jnp.float32(-1e30)
                )

    def forward(h):
        q = qh[h]
        top = jnp.full((1, TOK), -1e30, jnp.float32)
        for j in range(BLOCKS):
            x = lax.dot_general(kv[j, 0], q, NT, preferred_element_type=jnp.float32)
            x = x * (SCALE * LOG2E) + bias[j * TOK : (j + 1) * TOK, :]
            xbuf[j * TOK : (j + 1) * TOK, :] = x
            top = jnp.maximum(top, jnp.max(x, axis=0, keepdims=True))
        total = jnp.zeros((1, TOK), jnp.float32)
        out = jnp.zeros((HEAD, TOK), jnp.float32)
        for j in range(BLOCKS):
            e = jnp.exp2(xbuf[j * TOK : (j + 1) * TOK, :] - top)
            total = total + jnp.sum(e, axis=0, keepdims=True)
            low = e.astype(jnp.bfloat16)
            ebuf[h, j * TOK : (j + 1) * TOK, :] = low
            out = out + mm(kv_t[1, :, j * TOK : (j + 1) * TOK], low)
        inv = 1.0 / total
        rinv[h] = jnp.broadcast_to(inv, (8, TOK))
        att[h] = (out * inv).astype(jnp.bfloat16)

    def backward(h):
        att_h = att[h]
        go = jnp.zeros((HEAD, TOK), jnp.float32)
        for d in range(8):
            w = wbuf[h, d]
            go = go + mm(w, cot_t[d * 512 : (d + 1) * 512, :])
            gw = mm(att_h, cot[:, d * 512 : (d + 1) * 512])
            pacc[d % 2, d // 2, pl.ds(h, 1), :] = jnp.sum(
                gw * w.astype(jnp.float32), axis=0, keepdims=True
            )
        go = go * rinv[h, 0:1, :]
        delta = jnp.sum(go * att_h.astype(jnp.float32), axis=0, keepdims=True)
        go_low = go.astype(jnp.bfloat16)
        go_t = jnp.transpose(go).astype(jnp.bfloat16)
        q = qh[h]
        dq = jnp.zeros((HEAD, TOK), jnp.float32)
        for j in range(BLOCKS):
            part = slice(j * TOK, (j + 1) * TOK)
            e = ebuf[h, part, :]
            dprob = mm(kv[j, 1], go_low)
            ds = (e.astype(jnp.float32) * (dprob - delta)).astype(jnp.bfloat16)
            dq = dq + mm(kv_t[0, :, part], ds)
            dkv[0, part, :] += mm(ds, q)
            dkv[1, part, :] += mm(e, go_t)
        dq_ref[h] = jnp.transpose(dq * SCALE).astype(jnp.bfloat16)

    def step(i, _):
        @pl.when(i < HEADS)
        def _():
            @pl.when(i + 2 < HEADS)
            def _():
                z_start(i + 2)

            z_arrive(i)
            ycopy(i, 0).start()
            ycopy(i, 1).start()
            pcopy(i, 0).start()

            @pl.when(i == 0)
            def _():
                attention_inputs()

            forward(i)

        @pl.when((i >= AHEAD) & (i < HEADS + AHEAD))
        def _():
            c = i - AHEAD
            ycopy(c, 0).wait_recv()
            fcopy(c, 0).start()
            pcopy(c, 1).start()
            ycopy(c, 1).wait_recv()
            fcopy(c, 1).start()
            pcopy(c, 2).start()

        @pl.when(i >= AHEAD + 1)
        def _():
            c = i - AHEAD - 1
            fcopy(c, 0).wait_recv()
            fcopy(c, 1).wait_recv()
            pcopy(c, 3).start()
            for k in range(4):
                pcopy(c, k).wait_recv()
            backward(c)

        return 0

    lax.fori_loop(0, HEADS + AHEAD + 1, step, 0)

    def d_copy(k, to):
        return remote(dsend.at[k], drecv.at[k], gs_s.at[k], gs_r.at[k], seq=to)

    for k in range(2):
        part = slice((1 - k) * TOK, (2 - k) * TOK)
        dsend[k, 0] = dkv[0, part, :].astype(jnp.bfloat16)
        dsend[k, 1] = dkv[1, part, :].astype(jnp.bfloat16)

        @pl.when(s - 1 - k >= 0)
        def _():
            d_copy(k, s - 1 - k).start()

        @pl.when(s + 1 + k >= 4)
        def _():
            drecv[k] = jnp.zeros((2, TOK, HEAD), jnp.bfloat16)

    first = remote(pacc.at[1 - core], r1, s1, t1, dp=partner)
    first.start()
    first.wait_recv()
    p1[...] = pacc[core] + r1[...]

    def second(k):
        to = lax.rem(s + 1 + k, 4)
        return remote(p1.at[:, :, rows(to)], r2.at[k], s2.at[k], t2.at[k], seq=to)

    for k in range(3):
        second(k).start()
    mine = p1[:, :, rows(s)]
    for k in range(3):
        second(k).wait_recv()
        mine = mine + r2[k]
    p2[...] = mine

    def third(k):
        to = lax.rem(y + 1 + k, 4)
        return remote(p2.at[to], r3.at[k], s3.at[k], t3.at[k], dp=to * 2 + core)

    for k in range(3):
        third(k).start()
    total = p2[y]
    for k in range(3):
        third(k).wait_recv()
        total = total + r3[k]
    gs_ref[...] = total * STEP_SCALE / step_ref[...].astype(jnp.float32)

    for k in range(2):
        @pl.when(s + 1 + k < 4)
        def _():
            d_copy(k, s + 1 + k).wait_recv()

    own = slice(2 * TOK, 3 * TOK)
    recv = drecv[...].astype(jnp.float32)
    dk_ref[...] = ((dkv[0, own, :] + recv[0, 0] + recv[1, 0]) * SCALE).astype(jnp.bfloat16)
    dv_ref[...] = (dkv[1, own, :] + recv[0, 1] + recv[1, 1]).astype(jnp.bfloat16)

    def sent(c, _):
        for to in range(4):
            @pl.when(near(to))
            def _():
                zcopy(c, s, to, zs.at[c, to]).wait_send()

        @pl.when(s == 2)
        def _():
            zcopy(c, 0, 3, zf.at[c]).wait_send()

        @pl.when(s == 1)
        def _():
            zcopy(c, 3, 0, zf.at[c]).wait_send()

        for k in range(2):
            ycopy(c, k).wait_send()
            fcopy(c, k).wait_send()
        for k in range(4):
            pcopy(c, k).wait_send()
        return 0

    lax.fori_loop(0, HEADS, sent, 0)
    for k in range(2):
        @pl.when(s + 1 + k < 4)
        def _():
            seg_copy(k).wait_send()
            kv_copy(k).wait_send()

        @pl.when(s - 1 - k >= 0)
        def _():
            d_copy(k, s - 1 - k).wait_send()

    first.wait_send()
    for k in range(3):
        second(k).wait_send()
        third(k).wait_send()


def local(queries, keys, values, segment_ids, codes, zero_points, step_sizes, cotangent):
    bf16, f32, i32 = jnp.bfloat16, jnp.float32, jnp.int32
    dma = pltpu.SemaphoreType.DMA
    vmem = pltpu.VMEM
    in_vmem = pl.BlockSpec(memory_space=pltpu.VMEM)
    anywhere = pl.BlockSpec(memory_space=pl.ANY)
    steps, dq, dk, dv = pl.pallas_call(
        kernel,
        out_shape=(
            jax.ShapeDtypeStruct((HEADS, 128), f32),
            jax.ShapeDtypeStruct((HEADS, TOK, HEAD), bf16),
            jax.ShapeDtypeStruct((TOK, HEAD), bf16),
            jax.ShapeDtypeStruct((TOK, HEAD), bf16),
        ),
        in_specs=[anywhere, in_vmem, in_vmem, in_vmem, anywhere, in_vmem, in_vmem, anywhere],
        out_specs=(in_vmem, in_vmem, in_vmem, in_vmem),
        scratch_shapes=[
            vmem((TOK, HEADS, HEAD), bf16),
            vmem((TOK * HEADS, HEAD), f32),
            vmem((128, HEADS * HEAD), i32),
            vmem((TOK, DOUT), bf16),
            vmem((DOUT, TOK), bf16),
            vmem((HEADS, 8, HEAD, 512), bf16),
            vmem((BLOCKS, 2, TOK, HEAD), bf16),
            vmem((2, HEAD, BLOCKS * TOK), bf16),
            vmem((BLOCKS, 8, TOK), i32),
            vmem((BLOCKS * TOK, TOK), f32),
            vmem((HEADS, TOK, HEAD), bf16),
            vmem((BLOCKS * TOK, TOK), f32),
            vmem((HEADS, BLOCKS * TOK, TOK), bf16),
            vmem((HEADS, HEAD, TOK), bf16),
            vmem((HEADS, 8, TOK), f32),
            vmem((2, 4, HEADS, 512), f32),
            vmem((2, BLOCKS * TOK, HEAD), f32),
            vmem((4, HEADS, 512), f32),
            vmem((4, HEADS, 512), f32),
            vmem((4, HEADS, 128), f32),
            vmem((3, 4, HEADS, 128), f32),
            vmem((3, HEADS, 128), f32),
            vmem((2, 2, TOK, HEAD), bf16),
            vmem((2, 2, TOK, HEAD), bf16),
            dma((3,)),
            dma((HEADS, 4)), dma((HEADS, 4)), dma((HEADS,)),
            dma((HEADS, 2)), dma((HEADS, 2)), dma((HEADS, 2)), dma((HEADS, 2)),
            dma((HEADS, 4)), dma((HEADS, 4)),
            dma((2,)), dma((2,)), dma((2,)), dma((2,)),
            dma, dma, dma((3,)), dma((3,)), dma((3,)), dma((3,)),
            dma((2,)), dma((2,)),
        ],
        compiler_params=pltpu.CompilerParams(
            collective_id=0, has_side_effects=True, vmem_limit_bytes=56 * 2**20
        ),
        name="fused",
    )(
        queries[0], keys.reshape(TOK, HEAD), values.reshape(TOK, HEAD), segment_ids,
        codes, zero_points.T, step_sizes.T, cotangent[0],
    )
    grad_queries = jnp.transpose(dq, (1, 0, 2))[None]
    return (steps.T, grad_queries, dk.reshape(1, TOK, 1, HEAD), dv.reshape(1, TOK, 1, HEAD))


def solution(mesh):
    in_specs = (
        P("dp", "seq", "tensor", None),
        P("dp", "seq", "tensor", None),
        P("dp", "seq", "tensor", None),
        P("dp", "seq"),
        P(("dp", "seq"), "tensor"),
        P(("dp", "seq"), "tensor"),
        P(("dp", "seq"), "tensor"),
        P("dp", "seq", None),
    )
    out_specs = (
        P(("dp", "seq"), "tensor"),
        P("dp", "seq", "tensor", None),
        P("dp", "seq", "tensor", None),
        P("dp", "seq", "tensor", None),
    )
    return jax.shard_map(local, mesh=mesh, in_specs=in_specs, out_specs=out_specs, check_vma=False)
```

```python
import jax
import jax.numpy as jnp
from jax import lax
from jax.experimental import pallas as pl
from jax.experimental.pallas import tpu as pltpu
from jax.sharding import PartitionSpec as P

MESH = pl.DeviceIdType.MESH
HEADS = 8
HEAD = 128
TOK = 256
DOUT = 4096
BLOCKS = 3
WAYS = 7
SCALE = HEAD**-0.5
LOG2E = 1.4426950408889634
STEP_SCALE = 8192**-0.5
NT = (((1,), (1,)), ((), ()))


def mm(a, b):
    return jnp.dot(a, b, preferred_element_type=jnp.float32)


def kernel(
    q_hbm, k_ref, v_ref, seg_ref, codes_hbm, zero_ref, step_ref, cot_hbm,
    gs_ref, dq_ref, dk_ref, dv_ref,
    q_in, q_f32, codes, cot, cot_t, wbuf, kv, kv_t, seg, bias, qh, xbuf, ebuf, att, rinv, pacc, dkv,
    p1, r1, p2, r2, r3, dsend, drecv,
    in_sem, zs, zr, os, ors, ys, yr, fs, fr, ps, pr, kvs, kvr, sgs, sgr, s1, t1, s2, t2, s3, t3, gs_s, gs_r,
):
    dp = lax.axis_index("dp")
    s = lax.axis_index("seq")
    core = lax.rem(dp, 2)
    y = dp // 2
    partner = dp + 1 - 2 * core
    yp = lax.rem(y + 1, 4)
    ym = lax.rem(y + 3, 4)
    y2 = lax.rem(y + 2, 4)

    in_codes = pltpu.make_async_copy(codes_hbm, codes, in_sem.at[0])
    in_q = pltpu.make_async_copy(q_hbm, q_in, in_sem.at[1])
    in_cot = pltpu.make_async_copy(cot_hbm, cot, in_sem.at[2])
    in_codes.start()
    in_q.start()

    def cot_piece(d, slot):
        source = pl.multiple_of(d * 512 + lax.rem(slot + s, 4) * 128, 128)
        target = pl.multiple_of(d * 512 + slot * 128, 128)
        return pltpu.make_async_copy(
            cot_hbm.at[:, pl.ds(source, 128)], cot.at[:, pl.ds(target, 128)], in_sem.at[2]
        )

    def cot_start(d, _):
        for slot in range(4):
            cot_piece(d, slot).start()
        return 0


    barrier = pltpu.get_barrier_semaphore()
    for other in (partner, yp * 2 + core, ym * 2 + core, y2 * 2 + core):
        pl.semaphore_signal(barrier, inc=1, device_id={"dp": other}, device_id_type=MESH)
    for k in (1, 2, 3):
        pl.semaphore_signal(
            barrier, inc=1, device_id={"seq": lax.rem(s + k, 4)}, device_id_type=MESH
        )

    def remote(src, dst, send, recv, **to):
        return pltpu.make_async_remote_copy(
            src, dst, send, recv, device_id=to, device_id_type=MESH
        )

    def zcopy(c, slot, to, to_slot, send):
        return remote(
            wbuf.at[c, core, y, slot], wbuf.at[c, core, y, to_slot], send, zr.at[c, to_slot], seq=to
        )

    def bcopy(slot, to, to_slot, send):
        c = WAYS
        return remote(
            wbuf.at[c, core, :, slot], wbuf.at[c, core, :, to_slot], send, zr.at[c, to_slot], seq=to
        )

    def ycopy(c, k):
        part = wbuf.at[c, core, y, pl.ds(1, 3)]
        return remote(part, part, ys.at[c, k], yr.at[c, k], dp=(yp, ym)[k] * 2 + core)

    def ocopy(c, k):
        part = wbuf.at[c, core, y, 0]
        return remote(part, part, os.at[c, k], ors.at[c, k], dp=(yp, ym)[k] * 2 + core)

    def fcopy(c, k):
        part = wbuf.at[c, core, (ym, yp)[k], pl.ds(k * 2, 2)]
        return remote(part, part, fs.at[c, k], fr.at[c, k], dp=(yp, ym)[k] * 2 + core)

    def hcopy(k):
        part = wbuf.at[WAYS, core, (ym, yp)[k], 0, pl.ds(k * 64, 64)]
        return remote(part, part, fs.at[WAYS, k], fr.at[WAYS, k], dp=(yp, ym)[k] * 2 + core)

    def pcopy(c, k):
        part = wbuf.at[c, core, (y, ym, yp, y2)[k]]
        return remote(part, part, ps.at[c, k], pr.at[c, k], dp=partner)

    def wcopy():
        part = wbuf.at[WAYS, core]
        return remote(part, part, ps.at[WAYS, 0], pr.at[WAYS, 0], dp=partner)

    def near(to):
        return (jnp.abs(s - to) == 1) | (jnp.abs(s - to) == 2)

    inner = (s == 1) | (s == 2)
    end = jnp.where(s == 2, 3, 0)
    end_slot = jnp.where(s == 2, 1, 3)

    def own_start(c):
        for k in range(2):
            ocopy(c, k).start()

    def z_start(copy):
        for to in range(4):
            @pl.when(near(to))
            def _():
                copy(0, to, lax.rem(s + 4 - to, 4), to).start()

    def z_arrive(copy):
        @pl.when(inner)
        def _():
            copy(0, s, 2, 0).wait_recv()
            copy(2, end, end_slot, 4).start()

        for slot in range(1, 4):
            def wait():
                copy(0, s, slot, 0).wait_recv()

            if slot == 2:
                pl.when(jnp.logical_not(inner))(wait)
            else:
                wait()

    def way_a(c):
        return lambda slot, to, to_slot, k: zcopy(c, slot, to, to_slot, zs.at[c, k])

    def way_b(slot, to, to_slot, k):
        return bcopy(slot, to, to_slot, zs.at[WAYS, k])

    def make_weight(h):
        part = jnp.transpose(codes[:, h * HEAD : (h + 1) * HEAD].astype(jnp.float32))
        zero = zero_ref[h : h + 1, :].astype(jnp.float32)
        step = step_ref[...].astype(jnp.float32)[h : h + 1, :]
        wbuf[h, core, y, 0] = ((part - zero) * step).astype(jnp.bfloat16)

    def kv_copy(k):
        return remote(kv.at[2], kv.at[1 - k], kvs.at[k], kvr.at[k], seq=s + 1 + k)

    def seg_copy(k):
        return remote(seg.at[2], seg.at[1 - k], sgs.at[k], sgr.at[k], seq=s + 1 + k)

    in_codes.wait()
    make_weight(0)
    pl.semaphore_wait(barrier, 7)
    z_start(way_a(0))
    own_start(0)
    make_weight(1)
    z_start(way_a(1))
    own_start(1)
    for h in (WAYS, *range(2, WAYS)):
        make_weight(h)
        own_start(h)
    lax.fori_loop(0, 8, cot_start, 0)

    def kv_start():
        kv[2, 0] = k_ref[...]
        kv[2, 1] = v_ref[...]
        seg[2] = jnp.broadcast_to(seg_ref[...], (8, TOK))
        for k in range(2):
            @pl.when(s + 1 + k < 4)
            def _():
                seg_copy(k).start()
                kv_copy(k).start()

            @pl.when(s - 1 - k < 0)
            def _():
                kv[1 - k] = jnp.zeros((2, TOK, HEAD), jnp.bfloat16)
                seg[1 - k] = jnp.full((8, TOK), -1, jnp.int32)

    def query_inputs():
        in_q.wait()
        q_f32[...] = q_in[...].astype(jnp.float32).reshape(TOK * HEADS, HEAD)
        for h in range(HEADS):
            qh[h] = q_f32[pl.ds(h, TOK, stride=HEADS), :].astype(jnp.bfloat16)
        dkv[...] = jnp.zeros((2, BLOCKS * TOK, HEAD), jnp.float32)

    def cot_inputs():
        in_cot.wait()

        def turn(i, _):
            part = cot[:, pl.ds(pl.multiple_of(i * 512, 512), 512)].astype(jnp.float32)
            cot_t[pl.ds(pl.multiple_of(i * 512, 512), 512), :] = jnp.transpose(part).astype(
                jnp.bfloat16
            )
            return 0

        lax.fori_loop(0, 8, turn, 0)

    def attention_inputs():
        for k in range(2):
            @pl.when(s - 1 - k >= 0)
            def _():
                remote(
                    kv.at[2], kv.at[1 - k], kvs.at[k], kvr.at[k], seq=s - 1 - k
                ).wait_recv()
                remote(
                    seg.at[2], seg.at[1 - k], sgs.at[k], sgr.at[k], seq=s - 1 - k
                ).wait_recv()

        own = seg_ref[...].astype(jnp.float32)
        for j in range(BLOCKS):
            kv_t[0, :, j * TOK : (j + 1) * TOK] = jnp.transpose(
                kv[j, 0].astype(jnp.float32)
            ).astype(jnp.bfloat16)
            kv_t[1, :, j * TOK : (j + 1) * TOK] = jnp.transpose(
                kv[j, 1].astype(jnp.float32)
            ).astype(jnp.bfloat16)
            for half in range(2):
                row = seg[j, 0:1, half * 128 : (half + 1) * 128].astype(jnp.float32)
                column = jnp.transpose(jnp.broadcast_to(row, (128, 128)))
                column = jnp.concatenate([column, column], axis=1)
                allowed = column == own
                if j == BLOCKS - 1:
                    key_pos = half * 128 + lax.broadcasted_iota(jnp.int32, (128, TOK), 0)
                    query_pos = lax.broadcasted_iota(jnp.int32, (128, TOK), 1)
                    allowed = allowed & (key_pos <= query_pos)
                bias[j * TOK + half * 128 : j * TOK + (half + 1) * 128, :] = jnp.where(
                    allowed, jnp.float32(0.0), jnp.float32(-1e30)
                )

    def forward(h):
        q = qh[h]
        top = jnp.full((1, TOK), -1e30, jnp.float32)
        for j in range(BLOCKS):
            x = lax.dot_general(kv[j, 0], q, NT, preferred_element_type=jnp.float32)
            x = x * (SCALE * LOG2E) + bias[j * TOK : (j + 1) * TOK, :]
            xbuf[j * TOK : (j + 1) * TOK, :] = x
            top = jnp.maximum(top, jnp.max(x, axis=0, keepdims=True))
        total = jnp.zeros((1, TOK), jnp.float32)
        out = jnp.zeros((HEAD, TOK), jnp.float32)
        for j in range(BLOCKS):
            e = jnp.exp2(xbuf[j * TOK : (j + 1) * TOK, :] - top)
            total = total + jnp.sum(e, axis=0, keepdims=True)
            low = e.astype(jnp.bfloat16)
            ebuf[h, j * TOK : (j + 1) * TOK, :] = low
            out = out + mm(kv_t[1, :, j * TOK : (j + 1) * TOK], low)
        inv = 1.0 / total
        rinv[h] = jnp.broadcast_to(inv, (8, TOK))
        att[h] = (out * inv).astype(jnp.bfloat16)

    def d_copy(k, to):
        return remote(dsend.at[k], drecv.at[k], gs_s.at[k], gs_r.at[k], seq=to)

    def d_start(k):
        part = slice((1 - k) * TOK, (2 - k) * TOK)
        dsend[k, 0] = dkv[0, part, :].astype(jnp.bfloat16)
        dsend[k, 1] = dkv[1, part, :].astype(jnp.bfloat16)

        @pl.when(s - 1 - k >= 0)
        def _():
            d_copy(k, s - 1 - k).start()

        @pl.when(s + 1 + k >= 4)
        def _():
            drecv[k] = jnp.zeros((2, TOK, HEAD), jnp.bfloat16)

    first = remote(pacc.at[1 - core], r1, s1, t1, dp=partner)

    def second(k):
        to = lax.rem(s + 1 + k, 4)
        return remote(p1.at[:, :, pl.ds((1 + k) * 128, 128)], r2.at[k], s2.at[k], t2.at[k], seq=to)

    def third(k):
        to = lax.rem(y + 1 + k, 4)
        return remote(p2.at[to], r3.at[k], s3.at[k], t3.at[k], dp=to * 2 + core)

    def after_first():
        first.wait_recv()
        p1[...] = pacc[core] + r1[...]
        for k in range(3):
            second(k).start()

    def after_second():
        mine = p1[:, :, 0:128]
        for k in range(3):
            second(k).wait_recv()
            mine = mine + r2[k]
        p2[...] = mine
        for k in range(3):
            third(k).start()

    def weight_block(h, d):
        return jnp.concatenate([wbuf[h, d % 2, d // 2, b] for b in range(4)], axis=1)

    def backward(h):
        last = h == WAYS - 1
        att_h = att[h]
        for d in range(8):
            gw = mm(att_h, cot[:, d * 512 : (d + 1) * 512])
            pacc[d % 2, d // 2, pl.ds(h, 1), :] = jnp.sum(
                gw * weight_block(h, d).astype(jnp.float32), axis=0, keepdims=True
            )

        @pl.when(last)
        def _():
            first.start()

        go = jnp.zeros((HEAD, TOK), jnp.float32)
        for d in range(8):
            go = go + mm(weight_block(h, d), cot_t[d * 512 : (d + 1) * 512, :])
        go = go * rinv[h, 0:1, :]
        delta = jnp.sum(go * att_h.astype(jnp.float32), axis=0, keepdims=True)
        go_low = go.astype(jnp.bfloat16)
        go_t = jnp.transpose(go).astype(jnp.bfloat16)
        q = qh[h]
        dq = jnp.zeros((HEAD, TOK), jnp.float32)
        for j in range(BLOCKS):
            part = slice(j * TOK, (j + 1) * TOK)
            e = ebuf[h, part, :]
            dprob = mm(kv[j, 1], go_low)
            ds = (e.astype(jnp.float32) * (dprob - delta)).astype(jnp.bfloat16)
            dq = dq + mm(kv_t[0, :, part], ds)
            dkv[0, part, :] += mm(ds, q)
            dkv[1, part, :] += mm(e, go_t)
            if j < 2:
                @pl.when(last)
                def _():
                    d_start(1 - j)
                    if j == 0:
                        after_first()
        q_f32[pl.ds(h, TOK, stride=HEADS), :] = jnp.transpose(dq * SCALE)

    def step(i, _):
        @pl.when(i < WAYS)
        def _():
            @pl.when(i + 2 < WAYS)
            def _():
                z_start(way_a(i + 2))

            @pl.when(i + 2 == WAYS)
            def _():
                for k in range(2):
                    hcopy(k).wait_recv()
                z_start(way_b)

            z_arrive(way_a(i))
            ycopy(i, 0).start()
            ycopy(i, 1).start()
            pcopy(i, 0).start()

            @pl.when(i == 0)
            def _():
                kv_start()
                query_inputs()

            @pl.when(i == 1)
            def _():
                for k in range(2):
                    ocopy(WAYS, k).wait_recv()
                    hcopy(k).start()
                cot_inputs()

        @pl.when(i == 2)
        def _():
            attention_inputs()

        @pl.when((i >= 2) & (i < HEADS + 2))
        def _():
            forward(i - 2)

        @pl.when((i >= 1) & (i < WAYS + 1))
        def _():
            c = i - 1
            for k in range(2):
                ocopy(c, k).wait_recv()
                ycopy(c, k).wait_recv()
                fcopy(c, k).start()
                pcopy(c, 1 + k).start()

        @pl.when((i >= 2) & (i < WAYS + 2))
        def _():
            c = i - 2
            fcopy(c, 0).wait_recv()
            fcopy(c, 1).wait_recv()
            pcopy(c, 3).start()

        @pl.when(i == WAYS)
        def _():
            z_arrive(way_b)
            wcopy().start()

        @pl.when((i >= 3) & (i != WAYS + 2))
        def _():
            c = jnp.where(i > WAYS + 2, WAYS - 1, i - 3)
            for k in range(4):
                pcopy(c, k).wait_recv()

        @pl.when(i == WAYS + 2)
        def _():
            wcopy().wait_recv()

        @pl.when(i >= 3)
        def _():
            backward(jnp.where(i > WAYS + 2, WAYS - 1, jnp.where(i == WAYS + 2, WAYS, i - 3)))

        return 0

    lax.fori_loop(0, HEADS + 3, step, 0)

    after_second()
    dq_ref[...] = q_f32[...].reshape(TOK, HEADS, HEAD).astype(jnp.bfloat16)
    total = p2[y]
    for k in range(3):
        third(k).wait_recv()
        total = total + r3[k]
    gs_ref[...] = total * STEP_SCALE / step_ref[...].astype(jnp.float32)

    for k in range(2):
        @pl.when(s + 1 + k < 4)
        def _():
            d_copy(k, s + 1 + k).wait_recv()

    own = slice(2 * TOK, 3 * TOK)
    recv = drecv[...].astype(jnp.float32)
    dk_ref[...] = ((dkv[0, own, :] + recv[0, 0] + recv[1, 0]) * SCALE).astype(jnp.bfloat16)
    dv_ref[...] = (dkv[1, own, :] + recv[0, 1] + recv[1, 1]).astype(jnp.bfloat16)

    def z_sent(copy):
        for to in range(4):
            @pl.when(near(to))
            def _():
                copy(0, to, lax.rem(s + 4 - to, 4), to).wait_send()

        @pl.when(inner)
        def _():
            copy(2, end, end_slot, 4).wait_send()

    def sent(c, _):
        z_sent(way_a(c))
        for k in range(2):
            ocopy(c, k).wait_send()
            ycopy(c, k).wait_send()
            fcopy(c, k).wait_send()
        for k in range(4):
            pcopy(c, k).wait_send()
        return 0

    lax.fori_loop(0, WAYS, sent, 0)
    z_sent(way_b)
    for k in range(2):
        ocopy(WAYS, k).wait_send()
        hcopy(k).wait_send()
    wcopy().wait_send()
    for k in range(2):
        @pl.when(s + 1 + k < 4)
        def _():
            seg_copy(k).wait_send()
            kv_copy(k).wait_send()

        @pl.when(s - 1 - k >= 0)
        def _():
            d_copy(k, s - 1 - k).wait_send()

    first.wait_send()
    for k in range(3):
        second(k).wait_send()
        third(k).wait_send()


def hand_over(*refs):
    for k in range(4):
        refs[4 + k][...] = refs[k][...]


def local(queries, keys, values, segment_ids, codes, zero_points, step_sizes, cotangent):
    bf16, f32, i32 = jnp.bfloat16, jnp.float32, jnp.int32
    dma = pltpu.SemaphoreType.DMA
    vmem = pltpu.VMEM
    in_vmem = pl.BlockSpec(memory_space=pltpu.VMEM)
    anywhere = pl.BlockSpec(memory_space=pl.ANY)
    results = pl.pallas_call(
        kernel,
        out_shape=(
            jax.ShapeDtypeStruct((HEADS, 128), f32),
            jax.ShapeDtypeStruct((TOK, HEADS, HEAD), bf16),
            jax.ShapeDtypeStruct((TOK, HEAD), bf16),
            jax.ShapeDtypeStruct((TOK, HEAD), bf16),
        ),
        in_specs=[anywhere, in_vmem, in_vmem, in_vmem, anywhere, in_vmem, in_vmem, anywhere],
        out_specs=(in_vmem, in_vmem, in_vmem, in_vmem),
        scratch_shapes=[
            vmem((TOK, HEADS, HEAD), bf16),
            vmem((TOK * HEADS, HEAD), f32),
            vmem((128, HEADS * HEAD), i32),
            vmem((TOK, DOUT), bf16),
            vmem((DOUT, TOK), bf16),
            vmem((HEADS, 2, 4, 4, HEAD, 128), bf16),
            vmem((BLOCKS, 2, TOK, HEAD), bf16),
            vmem((2, HEAD, BLOCKS * TOK), bf16),
            vmem((BLOCKS, 8, TOK), i32),
            vmem((BLOCKS * TOK, TOK), f32),
            vmem((HEADS, TOK, HEAD), bf16),
            vmem((BLOCKS * TOK, TOK), f32),
            vmem((HEADS, BLOCKS * TOK, TOK), bf16),
            vmem((HEADS, HEAD, TOK), bf16),
            vmem((HEADS, 8, TOK), f32),
            vmem((2, 4, HEADS, 512), f32),
            vmem((2, BLOCKS * TOK, HEAD), f32),
            vmem((4, HEADS, 512), f32),
            vmem((4, HEADS, 512), f32),
            vmem((4, HEADS, 128), f32),
            vmem((3, 4, HEADS, 128), f32),
            vmem((3, HEADS, 128), f32),
            vmem((2, 2, TOK, HEAD), bf16),
            vmem((2, 2, TOK, HEAD), bf16),
            dma((3,)),
            dma((HEADS, 5)), dma((HEADS, 4)),
            dma((HEADS, 2)), dma((HEADS, 2)), dma((HEADS, 2)), dma((HEADS, 2)), dma((HEADS, 2)), dma((HEADS, 2)),
            dma((HEADS, 4)), dma((HEADS, 4)),
            dma((2,)), dma((2,)), dma((2,)), dma((2,)),
            dma, dma, dma((3,)), dma((3,)), dma((3,)), dma((3,)),
            dma((2,)), dma((2,)),
        ],
        compiler_params=pltpu.CompilerParams(
            collective_id=0, has_side_effects=True, vmem_limit_bytes=56 * 2**20
        ),
        name="fused",
    )(
        queries[0], keys.reshape(TOK, HEAD), values.reshape(TOK, HEAD), segment_ids,
        codes, zero_points.T, step_sizes.T, cotangent[0],
    )
    steps, dq, dk, dv = pl.pallas_call(
        hand_over,
        out_shape=[jax.ShapeDtypeStruct(r.shape, r.dtype) for r in results],
        in_specs=[in_vmem] * 4,
        out_specs=[in_vmem] * 4,
        name="hand_over",
    )(*results)
    return (steps.T, dq[None], dk.reshape(1, TOK, 1, HEAD), dv.reshape(1, TOK, 1, HEAD))


def solution(mesh):
    in_specs = (
        P("dp", "seq", "tensor", None),
        P("dp", "seq", "tensor", None),
        P("dp", "seq", "tensor", None),
        P("dp", "seq"),
        P(("dp", "seq"), "tensor"),
        P(("dp", "seq"), "tensor"),
        P(("dp", "seq"), "tensor"),
        P("dp", "seq", None),
    )
    out_specs = (
        P(("dp", "seq"), "tensor"),
        P("dp", "seq", "tensor", None),
        P("dp", "seq", "tensor", None),
        P("dp", "seq", "tensor", None),
    )
    return jax.shard_map(local, mesh=mesh, in_specs=in_specs, out_specs=out_specs, check_vma=False)
```

```python
import jax
import jax.numpy as jnp
from jax import lax
from jax.experimental import pallas as pl
from jax.experimental.pallas import tpu as pltpu
from jax.sharding import PartitionSpec as P

MESH = pl.DeviceIdType.MESH
HEADS = 8
HEAD = 128
TOK = 256
DOUT = 4096
BLOCKS = 3
WAYS = 7
SCALE = HEAD**-0.5
LOG2E = 1.4426950408889634
STEP_SCALE = 8192**-0.5
NT = (((1,), (1,)), ((), ()))


def mm(a, b):
    return jnp.dot(a, b, preferred_element_type=jnp.float32)


def kernel(
    q_hbm, k_ref, v_ref, seg_ref, codes_hbm, zero_ref, step_ref, cot_hbm,
    gs_ref, dq_ref, dk_ref, dv_ref,
    q_in, q_f32, codes, cot, cot_t, wbuf, kv, kv_t, seg, bias, qh, xbuf, ebuf, att, rinv, gout, pacc, dkv,
    p1, r1, p2, r2, r3, dfar, dnear, rfar, rnear,
    in_sem, zs, zr, os, ors, ys, yr, fs, fr, ps, pr, kvs, kvr, sgs, sgr, s1, t1, s2, t2, s3, t3, ds_s, ds_r,
):
    dp = lax.axis_index("dp")
    s = lax.axis_index("seq")
    core = lax.rem(dp, 2)
    y = dp // 2
    partner = dp + 1 - 2 * core
    yp = lax.rem(y + 1, 4)
    ym = lax.rem(y + 3, 4)
    y2 = lax.rem(y + 2, 4)

    in_codes = pltpu.make_async_copy(codes_hbm, codes, in_sem.at[0])
    in_q = pltpu.make_async_copy(q_hbm, q_in, in_sem.at[1])
    in_cot = pltpu.make_async_copy(cot_hbm, cot, in_sem.at[2])
    in_codes.start()
    in_q.start()

    def cot_piece(d, slot):
        source = pl.multiple_of(d * 512 + lax.rem(slot + s, 4) * 128, 128)
        target = pl.multiple_of(d * 512 + slot * 128, 128)
        return pltpu.make_async_copy(
            cot_hbm.at[:, pl.ds(source, 128)], cot.at[:, pl.ds(target, 128)], in_sem.at[2]
        )

    def cot_start(d, _):
        for slot in range(4):
            cot_piece(d, slot).start()
        return 0


    barrier = pltpu.get_barrier_semaphore()
    for other in (partner, yp * 2 + core, ym * 2 + core, y2 * 2 + core):
        pl.semaphore_signal(barrier, inc=1, device_id={"dp": other}, device_id_type=MESH)
    for k in (1, 2, 3):
        pl.semaphore_signal(
            barrier, inc=1, device_id={"seq": lax.rem(s + k, 4)}, device_id_type=MESH
        )

    def remote(src, dst, send, recv, **to):
        return pltpu.make_async_remote_copy(
            src, dst, send, recv, device_id=to, device_id_type=MESH
        )

    def zcopy(c, slot, to, to_slot, send):
        return remote(
            wbuf.at[c, core, y, slot], wbuf.at[c, core, y, to_slot], send, zr.at[c, to_slot], seq=to
        )

    def bcopy(slot, to, to_slot, send):
        c = WAYS
        return remote(
            wbuf.at[c, core, :, slot], wbuf.at[c, core, :, to_slot], send, zr.at[c, to_slot], seq=to
        )

    def ycopy(c, k):
        part = wbuf.at[c, core, y, pl.ds(1, 3)]
        return remote(part, part, ys.at[c, k], yr.at[c, k], dp=(yp, ym)[k] * 2 + core)

    def ocopy(c, k):
        part = wbuf.at[c, core, y, 0]
        return remote(part, part, os.at[c, k], ors.at[c, k], dp=(yp, ym)[k] * 2 + core)

    def fcopy(c, k):
        part = wbuf.at[c, core, (ym, yp)[k], pl.ds(k * 2, 2)]
        return remote(part, part, fs.at[c, k], fr.at[c, k], dp=(yp, ym)[k] * 2 + core)

    def hcopy(k):
        part = wbuf.at[WAYS, core, (ym, yp)[k], 0, pl.ds(k * 64, 64)]
        return remote(part, part, fs.at[WAYS, k], fr.at[WAYS, k], dp=(yp, ym)[k] * 2 + core)

    def pcopy(c, k):
        part = wbuf.at[c, core, (y, ym, yp, y2)[k]]
        return remote(part, part, ps.at[c, k], pr.at[c, k], dp=partner)

    def wcopy():
        part = wbuf.at[WAYS, core]
        return remote(part, part, ps.at[WAYS, 0], pr.at[WAYS, 0], dp=partner)

    def near(to):
        return (jnp.abs(s - to) == 1) | (jnp.abs(s - to) == 2)

    inner = (s == 1) | (s == 2)
    end = jnp.where(s == 2, 3, 0)
    end_slot = jnp.where(s == 2, 1, 3)

    def own_start(c):
        for k in range(2):
            ocopy(c, k).start()

    def z_start(copy):
        for to in range(4):
            @pl.when(near(to))
            def _():
                copy(0, to, lax.rem(s + 4 - to, 4), to).start()

    def z_arrive(copy):
        @pl.when(inner)
        def _():
            copy(0, s, 2, 0).wait_recv()
            copy(2, end, end_slot, 4).start()

        for slot in range(1, 4):
            def wait():
                copy(0, s, slot, 0).wait_recv()

            if slot == 2:
                pl.when(jnp.logical_not(inner))(wait)
            else:
                wait()

    def way_a(c):
        return lambda slot, to, to_slot, k: zcopy(c, slot, to, to_slot, zs.at[c, k])

    def way_b(slot, to, to_slot, k):
        return bcopy(slot, to, to_slot, zs.at[WAYS, k])

    def make_weight(h):
        part = jnp.transpose(codes[:, h * HEAD : (h + 1) * HEAD].astype(jnp.float32))
        zero = zero_ref[h : h + 1, :].astype(jnp.float32)
        step = step_ref[...].astype(jnp.float32)[h : h + 1, :]
        wbuf[h, core, y, 0] = ((part - zero) * step).astype(jnp.bfloat16)

    def kv_copy(k):
        return remote(kv.at[2], kv.at[1 - k], kvs.at[k], kvr.at[k], seq=s + 1 + k)

    def seg_copy(k):
        return remote(seg.at[2], seg.at[1 - k], sgs.at[k], sgr.at[k], seq=s + 1 + k)

    in_codes.wait()
    make_weight(0)
    pl.semaphore_wait(barrier, 7)
    z_start(way_a(0))
    own_start(0)
    make_weight(1)
    z_start(way_a(1))
    own_start(1)
    for h in (WAYS, *range(2, WAYS)):
        make_weight(h)
        own_start(h)
    lax.fori_loop(0, 8, cot_start, 0)

    def kv_start():
        kv[2, 0] = k_ref[...]
        kv[2, 1] = v_ref[...]
        seg[2] = jnp.broadcast_to(seg_ref[...], (8, TOK))
        for k in range(2):
            @pl.when(s + 1 + k < 4)
            def _():
                seg_copy(k).start()
                kv_copy(k).start()

            @pl.when(s - 1 - k < 0)
            def _():
                kv[1 - k] = jnp.zeros((2, TOK, HEAD), jnp.bfloat16)
                seg[1 - k] = jnp.full((8, TOK), -1, jnp.int32)

    def query_inputs():
        in_q.wait()
        q_f32[...] = q_in[...].astype(jnp.float32).reshape(TOK * HEADS, HEAD)
        for h in range(HEADS):
            qh[h] = q_f32[pl.ds(h, TOK, stride=HEADS), :].astype(jnp.bfloat16)
        dkv[...] = jnp.zeros((2, BLOCKS * TOK, HEAD), jnp.float32)

    def cot_inputs():
        in_cot.wait()

        def turn(i, _):
            part = cot[:, pl.ds(pl.multiple_of(i * 512, 512), 512)].astype(jnp.float32)
            cot_t[pl.ds(pl.multiple_of(i * 512, 512), 512), :] = jnp.transpose(part).astype(
                jnp.bfloat16
            )
            return 0

        lax.fori_loop(0, 8, turn, 0)

    def attention_inputs():
        for k in range(2):
            @pl.when(s - 1 - k >= 0)
            def _():
                remote(
                    kv.at[2], kv.at[1 - k], kvs.at[k], kvr.at[k], seq=s - 1 - k
                ).wait_recv()
                remote(
                    seg.at[2], seg.at[1 - k], sgs.at[k], sgr.at[k], seq=s - 1 - k
                ).wait_recv()

        own = seg_ref[...].astype(jnp.float32)
        for j in range(BLOCKS):
            kv_t[0, :, j * TOK : (j + 1) * TOK] = jnp.transpose(
                kv[j, 0].astype(jnp.float32)
            ).astype(jnp.bfloat16)
            kv_t[1, :, j * TOK : (j + 1) * TOK] = jnp.transpose(
                kv[j, 1].astype(jnp.float32)
            ).astype(jnp.bfloat16)
            for half in range(2):
                row = seg[j, 0:1, half * 128 : (half + 1) * 128].astype(jnp.float32)
                column = jnp.transpose(jnp.broadcast_to(row, (128, 128)))
                column = jnp.concatenate([column, column], axis=1)
                allowed = column == own
                if j == BLOCKS - 1:
                    key_pos = half * 128 + lax.broadcasted_iota(jnp.int32, (128, TOK), 0)
                    query_pos = lax.broadcasted_iota(jnp.int32, (128, TOK), 1)
                    allowed = allowed & (key_pos <= query_pos)
                bias[j * TOK + half * 128 : j * TOK + (half + 1) * 128, :] = jnp.where(
                    allowed, jnp.float32(0.0), jnp.float32(-1e30)
                )

    def forward(h):
        q = qh[h]
        top = jnp.full((1, TOK), -1e30, jnp.float32)
        for j in range(BLOCKS):
            x = lax.dot_general(kv[j, 0], q, NT, preferred_element_type=jnp.float32)
            x = x * (SCALE * LOG2E) + bias[j * TOK : (j + 1) * TOK, :]
            xbuf[j * TOK : (j + 1) * TOK, :] = x
            top = jnp.maximum(top, jnp.max(x, axis=0, keepdims=True))
        total = jnp.zeros((1, TOK), jnp.float32)
        out = jnp.zeros((HEAD, TOK), jnp.float32)
        for j in range(BLOCKS):
            e = jnp.exp2(xbuf[j * TOK : (j + 1) * TOK, :] - top)
            total = total + jnp.sum(e, axis=0, keepdims=True)
            low = e.astype(jnp.bfloat16)
            ebuf[h, j * TOK : (j + 1) * TOK, :] = low
            out = out + mm(kv_t[1, :, j * TOK : (j + 1) * TOK], low)
        inv = 1.0 / total
        rinv[h] = jnp.broadcast_to(inv, (8, TOK))
        att[h] = (out * inv).astype(jnp.bfloat16)

    def far_copy(kind, to):
        return remote(dfar.at[kind], rfar.at[kind], ds_s.at[0, kind], ds_r.at[0, kind], seq=to)

    def near_copy(kind, to):
        return remote(dnear.at[kind], rnear.at[kind], ds_s.at[1, kind], ds_r.at[1, kind], seq=to)

    def far_start(kind):
        dfar[kind] = dkv[kind, 0:TOK, :].astype(jnp.bfloat16)

        @pl.when(s >= 2)
        def _():
            far_copy(kind, s - 1).start()

        @pl.when((s == 0) | (s == 3))
        def _():
            rfar[kind] = jnp.zeros((TOK, HEAD), jnp.bfloat16)

    def near_start(kind):
        @pl.when(inner)
        def _():
            far_copy(kind, s + 1).wait_recv()

        both = dkv[kind, TOK : 2 * TOK, :] + rfar[kind].astype(jnp.float32)
        dnear[kind] = both.astype(jnp.bfloat16)

        @pl.when(s >= 1)
        def _():
            near_copy(kind, s - 1).start()

        @pl.when(s == 3)
        def _():
            rnear[kind] = jnp.zeros((TOK, HEAD), jnp.bfloat16)

    def first(k):
        part = pacc.at[:, :, :, pl.ds((1 + k) * 128, 128)]
        return remote(part, r1.at[k], s1.at[k], t1.at[k], seq=lax.rem(s + 1 + k, 4))

    second = remote(p1.at[1 - core], r2, s2, t2, dp=partner)

    def third(k):
        to = lax.rem(y + 1 + k, 4)
        return remote(p2.at[to], r3.at[k], s3.at[k], t3.at[k], dp=to * 2 + core)

    def after_first():
        mine = pacc[:, :, :, 0:128]
        for k in range(3):
            first(k).wait_recv()
            mine = mine + r1[k]
        p1[...] = mine
        second.start()

    def after_second():
        second.wait_recv()
        p2[...] = p1[core] + r2[...]
        for k in range(3):
            third(k).start()

    def weight_block(h, d):
        return jnp.concatenate([wbuf[h, d % 2, d // 2, b] for b in range(4)], axis=1)

    def kv_all(k):
        return jnp.concatenate([kv[j, k] for j in range(BLOCKS)], axis=0)

    def group_sums(heads):
        att_h = jnp.concatenate([att[h] for h in heads], axis=0)
        for d in range(8):
            gw = mm(att_h, cot[:, d * 512 : (d + 1) * 512])
            for n, h in enumerate(heads):
                w = weight_block(h, d).astype(jnp.float32)
                pacc[d % 2, d // 2, pl.ds(h, 1), :] = jnp.sum(
                    gw[n * HEAD : (n + 1) * HEAD] * w, axis=0, keepdims=True
                )

    def grad_out(heads):
        go = jnp.zeros((len(heads) * HEAD, TOK), jnp.float32)
        for d in range(8):
            w = jnp.concatenate([weight_block(h, d) for h in heads], axis=0)
            go = go + mm(w, cot_t[d * 512 : (d + 1) * 512, :])
        for n, h in enumerate(heads):
            gout[h] = go[n * HEAD : (n + 1) * HEAD] * rinv[h, 0:1, :]

    def attention(h, last=False):
        go = gout[h]
        delta = jnp.sum(go * att[h].astype(jnp.float32), axis=0, keepdims=True)
        e = ebuf[h]
        dkv[1] += mm(e, jnp.transpose(go).astype(jnp.bfloat16))
        if last:
            far_start(1)
        dprob = mm(kv_all(1), go.astype(jnp.bfloat16))
        ds = (e.astype(jnp.float32) * (dprob - delta)).astype(jnp.bfloat16)
        dkv[0] += mm(ds, qh[h])
        if last:
            far_start(0)
            after_first()
            near_start(1)
        dq = mm(kv_t[0], ds)
        q_f32[pl.ds(h, TOK, stride=HEADS), :] = jnp.transpose(dq * SCALE)

    def step(i, _):
        @pl.when(i < WAYS)
        def _():
            @pl.when(i + 2 < WAYS)
            def _():
                z_start(way_a(i + 2))

            @pl.when(i + 2 == WAYS)
            def _():
                for k in range(2):
                    hcopy(k).wait_recv()
                z_start(way_b)

            z_arrive(way_a(i))
            ycopy(i, 0).start()
            ycopy(i, 1).start()
            pcopy(i, 0).start()

            @pl.when(i == 0)
            def _():
                kv_start()
                query_inputs()

            @pl.when(i == 1)
            def _():
                for k in range(2):
                    ocopy(WAYS, k).wait_recv()
                    hcopy(k).start()
                cot_inputs()

        @pl.when(i == 2)
        def _():
            attention_inputs()

        def forward_turn(h, _):
            forward(h)
            return 0

        first_forward = jnp.where(i < 4, 2 * i - 4, i)
        forwards = jnp.where((i < 2) | (i >= HEADS), 0, jnp.where(i < 4, 2, 1))
        lax.fori_loop(first_forward, first_forward + forwards, forward_turn, 0)

        @pl.when((i >= 1) & (i < WAYS + 1))
        def _():
            c = i - 1
            for k in range(2):
                ocopy(c, k).wait_recv()
                ycopy(c, k).wait_recv()
                fcopy(c, k).start()
                pcopy(c, 1 + k).start()

        @pl.when((i >= 2) & (i < WAYS + 2))
        def _():
            c = i - 2
            fcopy(c, 0).wait_recv()
            fcopy(c, 1).wait_recv()
            pcopy(c, 3).start()

        @pl.when(i == WAYS)
        def _():
            z_arrive(way_b)
            wcopy().start()

        @pl.when((i >= 3) & (i < WAYS + 2))
        def _():
            for k in range(4):
                pcopy(i - 3, k).wait_recv()

        @pl.when(i == WAYS + 1)
        def _():
            wcopy().wait_recv()

        @pl.when((i == 4) | (i == 6) | (i == 8))
        def _():
            heads = (jnp.where(i == 8, 5, i - 4), jnp.where(i == 8, 7, i - 3))
            group_sums(heads)
            grad_out(heads)

        def attention_turn(h, _):
            @pl.when(h == 4)
            def _():
                group_sums((h,))
                grad_out((h,))

            attention(h)
            return 0

        first_head = jnp.where(i == 9, 7, jnp.where(i == 8, 5, i - 4))
        count = jnp.where(i < 4, 0, jnp.where(i == 7, 2, 1))
        lax.fori_loop(first_head, first_head + count, attention_turn, 0)
        return 0

    lax.fori_loop(0, HEADS + 2, step, 0)

    final = WAYS - 1
    for k in range(4):
        pcopy(final, k).wait_recv()
    group_sums((final,))
    for k in range(3):
        first(k).start()
    grad_out((final,))
    attention(final, last=True)
    near_start(0)
    after_second()
    dq_ref[...] = q_f32[...].reshape(TOK, HEADS, HEAD).astype(jnp.bfloat16)
    total = p2[y]
    for k in range(3):
        third(k).wait_recv()
        total = total + r3[k]
    gs_ref[...] = total * STEP_SCALE / step_ref[...].astype(jnp.float32)

    def z_sent(copy):
        for to in range(4):
            @pl.when(near(to))
            def _():
                copy(0, to, lax.rem(s + 4 - to, 4), to).wait_send()

        @pl.when(inner)
        def _():
            copy(2, end, end_slot, 4).wait_send()

    def sent(c, _):
        z_sent(way_a(c))
        for k in range(2):
            ocopy(c, k).wait_send()
            ycopy(c, k).wait_send()
            fcopy(c, k).wait_send()
        for k in range(4):
            pcopy(c, k).wait_send()
        return 0

    lax.fori_loop(0, WAYS, sent, 0)
    z_sent(way_b)
    for k in range(2):
        ocopy(WAYS, k).wait_send()
        hcopy(k).wait_send()
    wcopy().wait_send()
    for k in range(2):
        @pl.when(s + 1 + k < 4)
        def _():
            seg_copy(k).wait_send()
            kv_copy(k).wait_send()

    for k in range(3):
        first(k).wait_send()
        third(k).wait_send()
    second.wait_send()

    own = slice(2 * TOK, 3 * TOK)
    for kind, scale, out_ref in ((1, 1.0, dv_ref), (0, SCALE, dk_ref)):
        @pl.when(s < 3)
        def _():
            near_copy(kind, s + 1).wait_recv()

        total = dkv[kind, own, :] + rnear[kind].astype(jnp.float32)
        out_ref[...] = (total * scale).astype(jnp.bfloat16)

        @pl.when(s >= 2)
        def _():
            far_copy(kind, s - 1).wait_send()

        @pl.when(s >= 1)
        def _():
            near_copy(kind, s - 1).wait_send()


def hand_over(*refs):
    for k in range(4):
        refs[4 + k][...] = refs[k][...]


def local(queries, keys, values, segment_ids, codes, zero_points, step_sizes, cotangent):
    bf16, f32, i32 = jnp.bfloat16, jnp.float32, jnp.int32
    dma = pltpu.SemaphoreType.DMA
    vmem = pltpu.VMEM
    in_vmem = pl.BlockSpec(memory_space=pltpu.VMEM)
    anywhere = pl.BlockSpec(memory_space=pl.ANY)
    results = pl.pallas_call(
        kernel,
        out_shape=(
            jax.ShapeDtypeStruct((HEADS, 128), f32),
            jax.ShapeDtypeStruct((TOK, HEADS, HEAD), bf16),
            jax.ShapeDtypeStruct((TOK, HEAD), bf16),
            jax.ShapeDtypeStruct((TOK, HEAD), bf16),
        ),
        in_specs=[anywhere, in_vmem, in_vmem, in_vmem, anywhere, in_vmem, in_vmem, anywhere],
        out_specs=(in_vmem, in_vmem, in_vmem, in_vmem),
        scratch_shapes=[
            vmem((TOK, HEADS, HEAD), bf16),
            vmem((TOK * HEADS, HEAD), f32),
            vmem((128, HEADS * HEAD), i32),
            vmem((TOK, DOUT), bf16),
            vmem((DOUT, TOK), bf16),
            vmem((HEADS, 2, 4, 4, HEAD, 128), bf16),
            vmem((BLOCKS, 2, TOK, HEAD), bf16),
            vmem((2, HEAD, BLOCKS * TOK), bf16),
            vmem((BLOCKS, 8, TOK), i32),
            vmem((BLOCKS * TOK, TOK), f32),
            vmem((HEADS, TOK, HEAD), bf16),
            vmem((BLOCKS * TOK, TOK), f32),
            vmem((HEADS, BLOCKS * TOK, TOK), bf16),
            vmem((HEADS, HEAD, TOK), bf16),
            vmem((HEADS, 8, TOK), f32),
            vmem((HEADS, HEAD, TOK), f32),
            vmem((2, 4, HEADS, 512), f32),
            vmem((2, BLOCKS * TOK, HEAD), f32),
            vmem((2, 4, HEADS, 128), f32),
            vmem((3, 2, 4, HEADS, 128), f32),
            vmem((4, HEADS, 128), f32),
            vmem((4, HEADS, 128), f32),
            vmem((3, HEADS, 128), f32),
            vmem((2, TOK, HEAD), bf16),
            vmem((2, TOK, HEAD), bf16),
            vmem((2, TOK, HEAD), bf16),
            vmem((2, TOK, HEAD), bf16),
            dma((3,)),
            dma((HEADS, 5)), dma((HEADS, 4)),
            dma((HEADS, 2)), dma((HEADS, 2)), dma((HEADS, 2)), dma((HEADS, 2)), dma((HEADS, 2)), dma((HEADS, 2)),
            dma((HEADS, 4)), dma((HEADS, 4)),
            dma((2,)), dma((2,)), dma((2,)), dma((2,)),
            dma((3,)), dma((3,)), dma, dma, dma((3,)), dma((3,)),
            dma((2, 2)), dma((2, 2)),
        ],
        compiler_params=pltpu.CompilerParams(
            collective_id=0, has_side_effects=True, vmem_limit_bytes=56 * 2**20
        ),
        name="fused",
    )(
        queries[0], keys.reshape(TOK, HEAD), values.reshape(TOK, HEAD), segment_ids,
        codes, zero_points.T, step_sizes.T, cotangent[0],
    )
    steps, dq, dk, dv = pl.pallas_call(
        hand_over,
        out_shape=[jax.ShapeDtypeStruct(r.shape, r.dtype) for r in results],
        in_specs=[in_vmem] * 4,
        out_specs=[in_vmem] * 4,
        name="hand_over",
    )(*results)
    return (steps.T, dq[None], dk.reshape(1, TOK, 1, HEAD), dv.reshape(1, TOK, 1, HEAD))


def solution(mesh):
    in_specs = (
        P("dp", "seq", "tensor", None),
        P("dp", "seq", "tensor", None),
        P("dp", "seq", "tensor", None),
        P("dp", "seq"),
        P(("dp", "seq"), "tensor"),
        P(("dp", "seq"), "tensor"),
        P(("dp", "seq"), "tensor"),
        P("dp", "seq", None),
    )
    out_specs = (
        P(("dp", "seq"), "tensor"),
        P("dp", "seq", "tensor", None),
        P("dp", "seq", "tensor", None),
        P("dp", "seq", "tensor", None),
    )
    return jax.shard_map(local, mesh=mesh, in_specs=in_specs, out_specs=out_specs, check_vma=False)
```

```python
import jax
import jax.numpy as jnp
from jax import lax
from jax.experimental import pallas as pl
from jax.experimental.pallas import tpu as pltpu
from jax.sharding import PartitionSpec as P

MESH = pl.DeviceIdType.MESH
HEADS = 8
HEAD = 128
TOK = 256
DOUT = 4096
BLOCKS = 3
WAYS = 7
SCALE = HEAD**-0.5
LOG2E = 1.4426950408889634
STEP_SCALE = 8192**-0.5
NT = (((1,), (1,)), ((), ()))


def mm(a, b):
    return jnp.dot(a, b, preferred_element_type=jnp.float32)


def kernel(
    q_hbm, k_ref, v_ref, seg_ref, codes_hbm, zero_ref, step_ref, cot_hbm,
    gs_ref, dq_ref, dk_ref, dv_ref,
    q_in, q_f32, codes, cot, cot_t, wbuf, kv, kv_t, seg, bias, qh, xbuf, ebuf, att, rinv, gout, pacc, dkv,
    p1, r1, p2, r2, r3, dfar, dnear, rfar, rnear,
    in_sem, zs, zr, os, ors, ys, yr, fs, fr, ps, pr, kvs, kvr, sgs, sgr, s1, t1, s2, t2, s3, t3, ds_s, ds_r,
):
    dp = lax.axis_index("dp")
    s = lax.axis_index("seq")
    core = lax.rem(dp, 2)
    y = dp // 2
    partner = dp + 1 - 2 * core
    yp = lax.rem(y + 1, 4)
    ym = lax.rem(y + 3, 4)
    y2 = lax.rem(y + 2, 4)

    in_codes = pltpu.make_async_copy(codes_hbm, codes, in_sem.at[0])
    in_q = pltpu.make_async_copy(q_hbm, q_in, in_sem.at[1])
    in_cot = pltpu.make_async_copy(cot_hbm, cot, in_sem.at[2])
    in_codes.start()
    in_q.start()

    def cot_piece(d, slot):
        source = pl.multiple_of(d * 512 + lax.rem(slot + s, 4) * 128, 128)
        target = pl.multiple_of(d * 512 + slot * 128, 128)
        return pltpu.make_async_copy(
            cot_hbm.at[:, pl.ds(source, 128)], cot.at[:, pl.ds(target, 128)], in_sem.at[2]
        )

    def cot_start(d, _):
        for slot in range(4):
            cot_piece(d, slot).start()
        return 0


    barrier = pltpu.get_barrier_semaphore()
    for other in (partner, yp * 2 + core, ym * 2 + core, y2 * 2 + core):
        pl.semaphore_signal(barrier, inc=1, device_id={"dp": other}, device_id_type=MESH)
    for k in (1, 2, 3):
        pl.semaphore_signal(
            barrier, inc=1, device_id={"seq": lax.rem(s + k, 4)}, device_id_type=MESH
        )

    def remote(src, dst, send, recv, **to):
        return pltpu.make_async_remote_copy(
            src, dst, send, recv, device_id=to, device_id_type=MESH
        )

    def zcopy(c, slot, to, to_slot, send):
        return remote(
            wbuf.at[c, core, y, slot], wbuf.at[c, core, y, to_slot], send, zr.at[c, to_slot], seq=to
        )

    def bcopy(slot, to, to_slot, send):
        c = WAYS
        return remote(
            wbuf.at[c, core, :, slot], wbuf.at[c, core, :, to_slot], send, zr.at[c, to_slot], seq=to
        )

    def ycopy(c, k):
        part = wbuf.at[c, core, y, pl.ds(1, 3)]
        return remote(part, part, ys.at[c, k], yr.at[c, k], dp=(yp, ym)[k] * 2 + core)

    def ocopy(c, k):
        part = wbuf.at[c, core, y, 0]
        return remote(part, part, os.at[c, k], ors.at[c, k], dp=(yp, ym)[k] * 2 + core)

    def fcopy(c, k):
        part = wbuf.at[c, core, (ym, yp)[k], pl.ds(k * 2, 2)]
        return remote(part, part, fs.at[c, k], fr.at[c, k], dp=(yp, ym)[k] * 2 + core)

    def hcopy(k):
        part = wbuf.at[WAYS, core, (ym, yp)[k], 0, pl.ds(k * 64, 64)]
        return remote(part, part, fs.at[WAYS, k], fr.at[WAYS, k], dp=(yp, ym)[k] * 2 + core)

    def pcopy(c, k):
        part = wbuf.at[c, core, (y, ym, yp, y2)[k]]
        return remote(part, part, ps.at[c, k], pr.at[c, k], dp=partner)

    def wcopy():
        part = wbuf.at[WAYS, core]
        return remote(part, part, ps.at[WAYS, 0], pr.at[WAYS, 0], dp=partner)

    def near(to):
        return (jnp.abs(s - to) == 1) | (jnp.abs(s - to) == 2)

    inner = (s == 1) | (s == 2)
    end = jnp.where(s == 2, 3, 0)
    end_slot = jnp.where(s == 2, 1, 3)

    def own_start(c):
        for k in range(2):
            ocopy(c, k).start()

    def z_start(copy):
        for to in range(4):
            @pl.when(near(to))
            def _():
                copy(0, to, lax.rem(s + 4 - to, 4), to).start()

    def z_pass(copy):
        @pl.when(inner)
        def _():
            copy(0, s, 2, 0).wait_recv()
            copy(2, end, end_slot, 4).start()

    def z_arrive(copy):
        for slot in range(1, 4):
            def wait():
                copy(0, s, slot, 0).wait_recv()

            if slot == 2:
                pl.when(jnp.logical_not(inner))(wait)
            else:
                wait()

    def way_a(c):
        return lambda slot, to, to_slot, k: zcopy(c, slot, to, to_slot, zs.at[c, k])

    def way_b(slot, to, to_slot, k):
        return bcopy(slot, to, to_slot, zs.at[WAYS, k])

    def make_weight(h):
        part = jnp.transpose(codes[:, h * HEAD : (h + 1) * HEAD].astype(jnp.float32))
        zero = zero_ref[h : h + 1, :].astype(jnp.float32)
        step = step_ref[...].astype(jnp.float32)[h : h + 1, :]
        wbuf[h, core, y, 0] = ((part - zero) * step).astype(jnp.bfloat16)

    def kv_copy(k):
        return remote(kv.at[2 - k], kv.at[1 - k], kvs.at[k], kvr.at[k], seq=s + 1)

    def seg_copy(k):
        return remote(seg.at[2 - k], seg.at[1 - k], sgs.at[k], sgr.at[k], seq=s + 1)

    def kv_send(k):
        @pl.when((s < 3) & (s >= k))
        def _():
            seg_copy(k).start()
            kv_copy(k).start()

    def kv_arrive(k):
        @pl.when(s >= 1 + k)
        def _():
            remote(kv.at[2 - k], kv.at[1 - k], kvs.at[k], kvr.at[k], seq=s - 1).wait_recv()
            remote(seg.at[2 - k], seg.at[1 - k], sgs.at[k], sgr.at[k], seq=s - 1).wait_recv()

    in_codes.wait()
    make_weight(0)
    pl.semaphore_wait(barrier, 7)
    z_start(way_a(0))
    own_start(0)
    make_weight(1)
    z_start(way_a(1))
    own_start(1)
    make_weight(2)
    z_start(way_a(2))
    own_start(2)
    for h in (WAYS, *range(3, WAYS)):
        make_weight(h)
        own_start(h)
    lax.fori_loop(0, 8, cot_start, 0)
    z_pass(way_a(0))
    z_pass(way_a(1))

    def kv_start():
        kv[2, 0] = k_ref[...]
        kv[2, 1] = v_ref[...]
        seg[2] = jnp.broadcast_to(seg_ref[...], (8, TOK))
        for k in range(2):
            @pl.when(s - 1 - k < 0)
            def _():
                kv[1 - k] = jnp.zeros((2, TOK, HEAD), jnp.bfloat16)
                seg[1 - k] = jnp.full((8, TOK), -1, jnp.int32)

        kv_send(0)

    def query_inputs():
        in_q.wait()
        q_f32[...] = q_in[...].astype(jnp.float32).reshape(TOK * HEADS, HEAD)
        for h in range(HEADS):
            qh[h] = q_f32[pl.ds(h, TOK, stride=HEADS), :].astype(jnp.bfloat16)
        dkv[...] = jnp.zeros((2, BLOCKS * TOK, HEAD), jnp.float32)

    def cot_inputs():
        in_cot.wait()

        def turn(i, _):
            part = cot[:, pl.ds(pl.multiple_of(i * 512, 512), 512)].astype(jnp.float32)
            cot_t[pl.ds(pl.multiple_of(i * 512, 512), 512), :] = jnp.transpose(part).astype(
                jnp.bfloat16
            )
            return 0

        lax.fori_loop(0, 8, turn, 0)

    def attention_inputs():
        kv_arrive(1)
        own = seg_ref[...].astype(jnp.float32)
        for j in range(BLOCKS):
            kv_t[0, :, j * TOK : (j + 1) * TOK] = jnp.transpose(
                kv[j, 0].astype(jnp.float32)
            ).astype(jnp.bfloat16)
            kv_t[1, :, j * TOK : (j + 1) * TOK] = jnp.transpose(
                kv[j, 1].astype(jnp.float32)
            ).astype(jnp.bfloat16)
            for half in range(2):
                row = seg[j, 0:1, half * 128 : (half + 1) * 128].astype(jnp.float32)
                column = jnp.transpose(jnp.broadcast_to(row, (128, 128)))
                column = jnp.concatenate([column, column], axis=1)
                allowed = column == own
                if j == BLOCKS - 1:
                    key_pos = half * 128 + lax.broadcasted_iota(jnp.int32, (128, TOK), 0)
                    query_pos = lax.broadcasted_iota(jnp.int32, (128, TOK), 1)
                    allowed = allowed & (key_pos <= query_pos)
                bias[j * TOK + half * 128 : j * TOK + (half + 1) * 128, :] = jnp.where(
                    allowed, jnp.float32(0.0), jnp.float32(-1e30)
                )

    def forward(h):
        q = qh[h]
        top = jnp.full((1, TOK), -1e30, jnp.float32)
        for j in range(BLOCKS):
            x = lax.dot_general(kv[j, 0], q, NT, preferred_element_type=jnp.float32)
            x = x * (SCALE * LOG2E) + bias[j * TOK : (j + 1) * TOK, :]
            xbuf[j * TOK : (j + 1) * TOK, :] = x
            top = jnp.maximum(top, jnp.max(x, axis=0, keepdims=True))
        total = jnp.zeros((1, TOK), jnp.float32)
        out = jnp.zeros((HEAD, TOK), jnp.float32)
        for j in range(BLOCKS):
            e = jnp.exp2(xbuf[j * TOK : (j + 1) * TOK, :] - top)
            total = total + jnp.sum(e, axis=0, keepdims=True)
            low = e.astype(jnp.bfloat16)
            ebuf[h, j * TOK : (j + 1) * TOK, :] = low
            out = out + mm(kv_t[1, :, j * TOK : (j + 1) * TOK], low)
        inv = 1.0 / total
        rinv[h] = jnp.broadcast_to(inv, (8, TOK))
        att[h] = (out * inv).astype(jnp.bfloat16)

    def far_copy(kind, to):
        return remote(dfar.at[kind], rfar.at[kind], ds_s.at[0, kind], ds_r.at[0, kind], seq=to)

    def near_copy(kind, to):
        return remote(dnear.at[kind], rnear.at[kind], ds_s.at[1, kind], ds_r.at[1, kind], seq=to)

    def far_start(kind):
        dfar[kind] = dkv[kind, 0:TOK, :].astype(jnp.bfloat16)

        @pl.when(s >= 2)
        def _():
            far_copy(kind, s - 1).start()

        @pl.when((s == 0) | (s == 3))
        def _():
            rfar[kind] = jnp.zeros((TOK, HEAD), jnp.bfloat16)

    def near_start(kind):
        @pl.when(inner)
        def _():
            far_copy(kind, s + 1).wait_recv()

        both = dkv[kind, TOK : 2 * TOK, :] + rfar[kind].astype(jnp.float32)
        dnear[kind] = both.astype(jnp.bfloat16)

        @pl.when(s >= 1)
        def _():
            near_copy(kind, s - 1).start()

        @pl.when(s == 3)
        def _():
            rnear[kind] = jnp.zeros((TOK, HEAD), jnp.bfloat16)

    def first(k):
        part = pacc.at[:, :, :, pl.ds((1 + k) * 128, 128)]
        return remote(part, r1.at[k], s1.at[k], t1.at[k], seq=lax.rem(s + 1 + k, 4))

    second = remote(p1.at[1 - core], r2, s2, t2, dp=partner)

    def third(k):
        to = lax.rem(y + 1 + k, 4)
        return remote(p2.at[to], r3.at[k], s3.at[k], t3.at[k], dp=to * 2 + core)

    def after_first():
        mine = pacc[:, :, :, 0:128]
        for k in range(3):
            first(k).wait_recv()
            mine = mine + r1[k]
        p1[...] = mine
        second.start()

    def after_second():
        second.wait_recv()
        p2[...] = p1[core] + r2[...]
        for k in range(3):
            third(k).start()

    def weight_block(h, d):
        return jnp.concatenate([wbuf[h, d % 2, d // 2, b] for b in range(4)], axis=1)

    def kv_all(k):
        return jnp.concatenate([kv[j, k] for j in range(BLOCKS)], axis=0)

    def group_sums(heads):
        att_h = jnp.concatenate([att[h] for h in heads], axis=0)
        for d in range(8):
            gw = mm(att_h, cot[:, d * 512 : (d + 1) * 512])
            for n, h in enumerate(heads):
                w = weight_block(h, d).astype(jnp.float32)
                pacc[d % 2, d // 2, pl.ds(h, 1), :] = jnp.sum(
                    gw[n * HEAD : (n + 1) * HEAD] * w, axis=0, keepdims=True
                )

    def grad_out(heads):
        go = jnp.zeros((len(heads) * HEAD, TOK), jnp.float32)
        for d in range(8):
            w = jnp.concatenate([weight_block(h, d) for h in heads], axis=0)
            go = go + mm(w, cot_t[d * 512 : (d + 1) * 512, :])
        for n, h in enumerate(heads):
            gout[h] = go[n * HEAD : (n + 1) * HEAD] * rinv[h, 0:1, :]

    def attention(h, last=False):
        go = gout[h]
        delta = jnp.sum(go * att[h].astype(jnp.float32), axis=0, keepdims=True)
        e = ebuf[h]
        dkv[1] += mm(e, jnp.transpose(go).astype(jnp.bfloat16))
        if last:
            far_start(1)
        dprob = mm(kv_all(1), go.astype(jnp.bfloat16))
        ds = (e.astype(jnp.float32) * (dprob - delta)).astype(jnp.bfloat16)
        dkv[0] += mm(ds, qh[h])
        if last:
            far_start(0)
            after_first()
            near_start(1)
        dq = mm(kv_t[0], ds)
        q_f32[pl.ds(h, TOK, stride=HEADS), :] = jnp.transpose(dq * SCALE)

    def y_start(c):
        z_arrive(way_a(c))
        ycopy(c, 0).start()
        ycopy(c, 1).start()
        pcopy(c, 0).start()

    y_start(0)

    def step(i, _):
        @pl.when(i < WAYS)
        def _():
            @pl.when(i + 3 < WAYS)
            def _():
                z_start(way_a(i + 3))

            @pl.when(i + 4 == WAYS)
            def _():
                for k in range(2):
                    hcopy(k).wait_recv()
                z_start(way_b)

            @pl.when(i + 2 < WAYS)
            def _():
                z_pass(way_a(i + 2))

            @pl.when(i + 1 == WAYS)
            def _():
                z_pass(way_b)

            @pl.when(i + 1 < WAYS)
            def _():
                y_start(i + 1)

            @pl.when(i == 0)
            def _():
                kv_start()
                query_inputs()

            @pl.when(i == 1)
            def _():
                for k in range(2):
                    ocopy(WAYS, k).wait_recv()
                    hcopy(k).start()
                cot_inputs()

        @pl.when((i >= 1) & (i < WAYS + 1))
        def _():
            c = i - 1
            for k in range(2):
                ocopy(c, k).wait_recv()
                ycopy(c, k).wait_recv()
                fcopy(c, k).start()
                pcopy(c, 1 + k).start()

        @pl.when((i >= 2) & (i < WAYS + 2))
        def _():
            c = i - 2
            fcopy(c, 0).wait_recv()
            fcopy(c, 1).wait_recv()
            pcopy(c, 3).start()

        @pl.when(i == 2)
        def _():
            kv_arrive(0)
            kv_send(1)

        @pl.when(i == 3)
        def _():
            attention_inputs()

        @pl.when(i == WAYS)
        def _():
            z_arrive(way_b)
            wcopy().start()

        def forward_turn(h, _):
            forward(h)
            return 0

        first_forward = jnp.where(i == 3, 0, jnp.where(i == 4, 4, 7))
        forwards = jnp.where(i == 3, 4, jnp.where(i == 4, 3, jnp.where(i == 5, 1, 0)))
        lax.fori_loop(first_forward, first_forward + forwards, forward_turn, 0)

        def attention_turn(n, _):
            attention(jnp.where(i == 8, 5 + 2 * n, jnp.where(i == 7, 4, i - 4 + n)))
            return 0

        count = jnp.where(i < 4, 0, jnp.where((i == 6) | (i == 8), 2, 1))
        lax.fori_loop(0, count, attention_turn, 0)

        @pl.when((i >= 2) & (i < WAYS + 1))
        def _():
            for k in range(4):
                pcopy(i - 2, k).wait_recv()

        @pl.when(i == WAYS)
        def _():
            wcopy().wait_recv()

        @pl.when((i == 3) | (i == 5) | (i == WAYS))
        def _():
            heads = (jnp.where(i == WAYS, 5, i - 3), jnp.where(i == WAYS, 7, i - 2))
            group_sums(heads)
            grad_out(heads)

        @pl.when(i == 6)
        def _():
            group_sums((4,))
            grad_out((4,))

        return 0

    lax.fori_loop(0, HEADS + 1, step, 0)

    final = WAYS - 1
    for k in range(4):
        pcopy(final, k).wait_recv()
    group_sums((final,))
    for k in range(3):
        first(k).start()
    grad_out((final,))
    attention(final, last=True)
    near_start(0)
    after_second()
    dq_ref[...] = q_f32[...].reshape(TOK, HEADS, HEAD).astype(jnp.bfloat16)
    total = p2[y]
    for k in range(3):
        third(k).wait_recv()
        total = total + r3[k]
    gs_ref[...] = total * STEP_SCALE / step_ref[...].astype(jnp.float32)

    def z_sent(copy):
        for to in range(4):
            @pl.when(near(to))
            def _():
                copy(0, to, lax.rem(s + 4 - to, 4), to).wait_send()

        @pl.when(inner)
        def _():
            copy(2, end, end_slot, 4).wait_send()

    def sent(c, _):
        z_sent(way_a(c))
        for k in range(2):
            ocopy(c, k).wait_send()
            ycopy(c, k).wait_send()
            fcopy(c, k).wait_send()
        for k in range(4):
            pcopy(c, k).wait_send()
        return 0

    lax.fori_loop(0, WAYS, sent, 0)
    z_sent(way_b)
    for k in range(2):
        ocopy(WAYS, k).wait_send()
        hcopy(k).wait_send()
    wcopy().wait_send()
    for k in range(2):
        @pl.when((s < 3) & (s >= k))
        def _():
            seg_copy(k).wait_send()
            kv_copy(k).wait_send()

    for k in range(3):
        first(k).wait_send()
        third(k).wait_send()
    second.wait_send()

    own = slice(2 * TOK, 3 * TOK)
    for kind, scale, out_ref in ((1, 1.0, dv_ref), (0, SCALE, dk_ref)):
        @pl.when(s < 3)
        def _():
            near_copy(kind, s + 1).wait_recv()

        total = dkv[kind, own, :] + rnear[kind].astype(jnp.float32)
        out_ref[...] = (total * scale).astype(jnp.bfloat16)

        @pl.when(s >= 2)
        def _():
            far_copy(kind, s - 1).wait_send()

        @pl.when(s >= 1)
        def _():
            near_copy(kind, s - 1).wait_send()


def hand_over(*refs):
    for k in range(4):
        refs[4 + k][...] = refs[k][...]


def local(queries, keys, values, segment_ids, codes, zero_points, step_sizes, cotangent):
    bf16, f32, i32 = jnp.bfloat16, jnp.float32, jnp.int32
    dma = pltpu.SemaphoreType.DMA
    vmem = pltpu.VMEM
    in_vmem = pl.BlockSpec(memory_space=pltpu.VMEM)
    anywhere = pl.BlockSpec(memory_space=pl.ANY)
    results = pl.pallas_call(
        kernel,
        out_shape=(
            jax.ShapeDtypeStruct((HEADS, 128), f32),
            jax.ShapeDtypeStruct((TOK, HEADS, HEAD), bf16),
            jax.ShapeDtypeStruct((TOK, HEAD), bf16),
            jax.ShapeDtypeStruct((TOK, HEAD), bf16),
        ),
        in_specs=[anywhere, in_vmem, in_vmem, in_vmem, anywhere, in_vmem, in_vmem, anywhere],
        out_specs=(in_vmem, in_vmem, in_vmem, in_vmem),
        scratch_shapes=[
            vmem((TOK, HEADS, HEAD), bf16),
            vmem((TOK * HEADS, HEAD), f32),
            vmem((128, HEADS * HEAD), i32),
            vmem((TOK, DOUT), bf16),
            vmem((DOUT, TOK), bf16),
            vmem((HEADS, 2, 4, 4, HEAD, 128), bf16),
            vmem((BLOCKS, 2, TOK, HEAD), bf16),
            vmem((2, HEAD, BLOCKS * TOK), bf16),
            vmem((BLOCKS, 8, TOK), i32),
            vmem((BLOCKS * TOK, TOK), f32),
            vmem((HEADS, TOK, HEAD), bf16),
            vmem((BLOCKS * TOK, TOK), f32),
            vmem((HEADS, BLOCKS * TOK, TOK), bf16),
            vmem((HEADS, HEAD, TOK), bf16),
            vmem((HEADS, 8, TOK), f32),
            vmem((HEADS, HEAD, TOK), f32),
            vmem((2, 4, HEADS, 512), f32),
            vmem((2, BLOCKS * TOK, HEAD), f32),
            vmem((2, 4, HEADS, 128), f32),
            vmem((3, 2, 4, HEADS, 128), f32),
            vmem((4, HEADS, 128), f32),
            vmem((4, HEADS, 128), f32),
            vmem((3, HEADS, 128), f32),
            vmem((2, TOK, HEAD), bf16),
            vmem((2, TOK, HEAD), bf16),
            vmem((2, TOK, HEAD), bf16),
            vmem((2, TOK, HEAD), bf16),
            dma((3,)),
            dma((HEADS, 5)), dma((HEADS, 4)),
            dma((HEADS, 2)), dma((HEADS, 2)), dma((HEADS, 2)), dma((HEADS, 2)), dma((HEADS, 2)), dma((HEADS, 2)),
            dma((HEADS, 4)), dma((HEADS, 4)),
            dma((2,)), dma((2,)), dma((2,)), dma((2,)),
            dma((3,)), dma((3,)), dma, dma, dma((3,)), dma((3,)),
            dma((2, 2)), dma((2, 2)),
        ],
        compiler_params=pltpu.CompilerParams(
            collective_id=0, has_side_effects=True, vmem_limit_bytes=56 * 2**20
        ),
        name="fused",
    )(
        queries[0], keys.reshape(TOK, HEAD), values.reshape(TOK, HEAD), segment_ids,
        codes, zero_points.T, step_sizes.T, cotangent[0],
    )
    steps, dq, dk, dv = pl.pallas_call(
        hand_over,
        out_shape=[jax.ShapeDtypeStruct(r.shape, r.dtype) for r in results],
        in_specs=[in_vmem] * 4,
        out_specs=[in_vmem] * 4,
        name="hand_over",
    )(*results)
    return (steps.T, dq[None], dk.reshape(1, TOK, 1, HEAD), dv.reshape(1, TOK, 1, HEAD))


def solution(mesh):
    in_specs = (
        P("dp", "seq", "tensor", None),
        P("dp", "seq", "tensor", None),
        P("dp", "seq", "tensor", None),
        P("dp", "seq"),
        P(("dp", "seq"), "tensor"),
        P(("dp", "seq"), "tensor"),
        P(("dp", "seq"), "tensor"),
        P("dp", "seq", None),
    )
    out_specs = (
        P(("dp", "seq"), "tensor"),
        P("dp", "seq", "tensor", None),
        P("dp", "seq", "tensor", None),
        P("dp", "seq", "tensor", None),
    )
    return jax.shard_map(local, mesh=mesh, in_specs=in_specs, out_specs=out_specs, check_vma=False)
```

```python
import jax
import jax.numpy as jnp
from jax import lax
from jax.experimental import pallas as pl
from jax.experimental.pallas import tpu as pltpu
from jax.sharding import PartitionSpec as P

MESH = pl.DeviceIdType.MESH
HEADS = 8
HEAD = 128
TOK = 256
DOUT = 4096
BLOCKS = 3
WAYS = 7
SCALE = HEAD**-0.5
LOG2E = 1.4426950408889634
STEP_SCALE = 8192**-0.5
NT = (((1,), (1,)), ((), ()))


def mm(a, b):
    return jnp.dot(a, b, preferred_element_type=jnp.float32)


def kernel(
    q_hbm, k_ref, v_ref, seg_ref, codes_hbm, zero_ref, step_ref, cot_hbm,
    gs_ref, dq_ref, dk_ref, dv_ref,
    q_in, q_f32, codes, cot, cot_t, wbuf, kv, kv_t, seg, bias, qh, xbuf, ebuf, att, rinv, gout, pacc, dkv,
    p1, r1, p2, r2, r3, dfar, dnear, rfar, rnear,
    in_sem, zs, zr, os, ors, ys, yr, fs, fr, ps, pr, kvs, kvr, sgs, sgr, s1, t1, s2, t2, s3, t3, ds_s, ds_r,
):
    dp = lax.axis_index("dp")
    s = lax.axis_index("seq")
    core = lax.rem(dp, 2)
    y = dp // 2
    partner = dp + 1 - 2 * core
    yp = lax.rem(y + 1, 4)
    ym = lax.rem(y + 3, 4)
    y2 = lax.rem(y + 2, 4)

    in_codes = pltpu.make_async_copy(codes_hbm, codes, in_sem.at[0])
    in_q = pltpu.make_async_copy(q_hbm, q_in, in_sem.at[1])
    in_cot = pltpu.make_async_copy(cot_hbm, cot, in_sem.at[2])
    in_codes.start()
    in_q.start()

    def cot_piece(d, slot):
        source = pl.multiple_of(d * 512 + lax.rem(slot + s, 4) * 128, 128)
        target = pl.multiple_of(d * 512 + slot * 128, 128)
        return pltpu.make_async_copy(
            cot_hbm.at[:, pl.ds(source, 128)], cot.at[:, pl.ds(target, 128)], in_sem.at[2]
        )

    def cot_start(d, _):
        for slot in range(4):
            cot_piece(d, slot).start()
        return 0


    barrier = pltpu.get_barrier_semaphore()
    for other in (partner, yp * 2 + core, ym * 2 + core, y2 * 2 + core):
        pl.semaphore_signal(barrier, inc=1, device_id={"dp": other}, device_id_type=MESH)
    for k in (1, 2, 3):
        pl.semaphore_signal(
            barrier, inc=1, device_id={"seq": lax.rem(s + k, 4)}, device_id_type=MESH
        )

    def remote(src, dst, send, recv, **to):
        return pltpu.make_async_remote_copy(
            src, dst, send, recv, device_id=to, device_id_type=MESH
        )

    def zcopy(c, slot, to, to_slot, send):
        return remote(
            wbuf.at[c, core, y, slot], wbuf.at[c, core, y, to_slot], send, zr.at[c, to_slot], seq=to
        )

    def bcopy(slot, to, to_slot, send):
        c = WAYS
        return remote(
            wbuf.at[c, core, :, slot], wbuf.at[c, core, :, to_slot], send, zr.at[c, to_slot], seq=to
        )

    def ycopy(c, k):
        part = wbuf.at[c, core, y, pl.ds(1, 3)]
        return remote(part, part, ys.at[c, k], yr.at[c, k], dp=(yp, ym)[k] * 2 + core)

    def ocopy(c, k):
        part = wbuf.at[c, core, y, 0]
        return remote(part, part, os.at[c, k], ors.at[c, k], dp=(yp, ym)[k] * 2 + core)

    def fcopy(c, k):
        part = wbuf.at[c, core, (ym, yp)[k], pl.ds(k * 2, 2)]
        return remote(part, part, fs.at[c, k], fr.at[c, k], dp=(yp, ym)[k] * 2 + core)

    def hcopy(k):
        part = wbuf.at[WAYS, core, (ym, yp)[k], 0, pl.ds(k * 64, 64)]
        return remote(part, part, fs.at[WAYS, k], fr.at[WAYS, k], dp=(yp, ym)[k] * 2 + core)

    def pcopy(c, k):
        part = wbuf.at[c, core, (y, ym, yp, y2)[k]]
        return remote(part, part, ps.at[c, k], pr.at[c, k], dp=partner)

    def wcopy():
        part = wbuf.at[WAYS, core]
        return remote(part, part, ps.at[WAYS, 0], pr.at[WAYS, 0], dp=partner)

    def near(to):
        return (jnp.abs(s - to) == 1) | (jnp.abs(s - to) == 2)

    inner = (s == 1) | (s == 2)
    end = jnp.where(s == 2, 3, 0)
    end_slot = jnp.where(s == 2, 1, 3)

    def own_start(c):
        for k in range(2):
            ocopy(c, k).start()

    def z_start(copy):
        for to in range(4):
            @pl.when(near(to))
            def _():
                copy(0, to, lax.rem(s + 4 - to, 4), to).start()

    def z_pass(copy):
        @pl.when(inner)
        def _():
            copy(0, s, 2, 0).wait_recv()
            copy(2, end, end_slot, 4).start()

    def z_arrive(copy):
        for slot in range(1, 4):
            def wait():
                copy(0, s, slot, 0).wait_recv()

            if slot == 2:
                pl.when(jnp.logical_not(inner))(wait)
            else:
                wait()

    def way_a(c):
        return lambda slot, to, to_slot, k: zcopy(c, slot, to, to_slot, zs.at[c, k])

    def way_b(slot, to, to_slot, k):
        return bcopy(slot, to, to_slot, zs.at[WAYS, k])

    def make_weight(h):
        part = jnp.transpose(codes[:, h * HEAD : (h + 1) * HEAD].astype(jnp.float32))
        zero = zero_ref[h : h + 1, :].astype(jnp.float32)
        step = step_ref[...].astype(jnp.float32)[h : h + 1, :]
        wbuf[h, core, y, 0] = ((part - zero) * step).astype(jnp.bfloat16)

    def kv_copy(k):
        return remote(kv.at[2 - k], kv.at[1 - k], kvs.at[k], kvr.at[k], seq=s + 1)

    def seg_copy(k):
        return remote(seg.at[2 - k], seg.at[1 - k], sgs.at[k], sgr.at[k], seq=s + 1)

    def kv_send(k):
        @pl.when((s < 3) & (s >= k))
        def _():
            seg_copy(k).start()
            kv_copy(k).start()

    def kv_arrive(k):
        @pl.when(s >= 1 + k)
        def _():
            remote(kv.at[2 - k], kv.at[1 - k], kvs.at[k], kvr.at[k], seq=s - 1).wait_recv()
            remote(seg.at[2 - k], seg.at[1 - k], sgs.at[k], sgr.at[k], seq=s - 1).wait_recv()

    in_codes.wait()
    make_weight(0)
    pl.semaphore_wait(barrier, 7)
    z_start(way_a(0))
    own_start(0)
    make_weight(1)
    z_start(way_a(1))
    own_start(1)
    make_weight(2)
    z_start(way_a(2))
    own_start(2)
    for h in (WAYS, *range(3, WAYS)):
        make_weight(h)
        own_start(h)
    lax.fori_loop(0, 8, cot_start, 0)
    z_pass(way_a(0))
    z_pass(way_a(1))

    def kv_start():
        kv[2, 0] = k_ref[...]
        kv[2, 1] = v_ref[...]
        seg[2] = jnp.broadcast_to(seg_ref[...], (8, TOK))
        for k in range(2):
            @pl.when(s - 1 - k < 0)
            def _():
                kv[1 - k] = jnp.zeros((2, TOK, HEAD), jnp.bfloat16)
                seg[1 - k] = jnp.full((8, TOK), -1, jnp.int32)

        kv_send(0)

    def query_inputs():
        in_q.wait()
        q_f32[...] = q_in[...].astype(jnp.float32).reshape(TOK * HEADS, HEAD)
        for h in range(HEADS):
            qh[h] = q_f32[pl.ds(h, TOK, stride=HEADS), :].astype(jnp.bfloat16)
        dkv[...] = jnp.zeros((2, BLOCKS * TOK, HEAD), jnp.float32)

    def cot_inputs():
        in_cot.wait()

        def turn(i, _):
            part = cot[:, pl.ds(pl.multiple_of(i * 512, 512), 512)].astype(jnp.float32)
            cot_t[pl.ds(pl.multiple_of(i * 512, 512), 512), :] = jnp.transpose(part).astype(
                jnp.bfloat16
            )
            return 0

        lax.fori_loop(0, 8, turn, 0)

    def attention_inputs():
        kv_arrive(1)
        own = seg_ref[...].astype(jnp.float32)
        for j in range(BLOCKS):
            kv_t[0, :, j * TOK : (j + 1) * TOK] = jnp.transpose(
                kv[j, 0].astype(jnp.float32)
            ).astype(jnp.bfloat16)
            kv_t[1, :, j * TOK : (j + 1) * TOK] = jnp.transpose(
                kv[j, 1].astype(jnp.float32)
            ).astype(jnp.bfloat16)
            for half in range(2):
                row = seg[j, 0:1, half * 128 : (half + 1) * 128].astype(jnp.float32)
                column = jnp.transpose(jnp.broadcast_to(row, (128, 128)))
                column = jnp.concatenate([column, column], axis=1)
                allowed = column == own
                if j == BLOCKS - 1:
                    key_pos = half * 128 + lax.broadcasted_iota(jnp.int32, (128, TOK), 0)
                    query_pos = lax.broadcasted_iota(jnp.int32, (128, TOK), 1)
                    allowed = allowed & (key_pos <= query_pos)
                bias[j * TOK + half * 128 : j * TOK + (half + 1) * 128, :] = jnp.where(
                    allowed, jnp.float32(0.0), jnp.float32(-1e30)
                )

    def forward(h):
        q = qh[h]
        top = jnp.full((1, TOK), -1e30, jnp.float32)
        for j in range(BLOCKS):
            x = lax.dot_general(kv[j, 0], q, NT, preferred_element_type=jnp.float32)
            x = x * (SCALE * LOG2E) + bias[j * TOK : (j + 1) * TOK, :]
            xbuf[j * TOK : (j + 1) * TOK, :] = x
            top = jnp.maximum(top, jnp.max(x, axis=0, keepdims=True))
        total = jnp.zeros((1, TOK), jnp.float32)
        out = jnp.zeros((HEAD, TOK), jnp.float32)
        for j in range(BLOCKS):
            e = jnp.exp2(xbuf[j * TOK : (j + 1) * TOK, :] - top)
            total = total + jnp.sum(e, axis=0, keepdims=True)
            low = e.astype(jnp.bfloat16)
            ebuf[h, j * TOK : (j + 1) * TOK, :] = low
            out = out + mm(kv_t[1, :, j * TOK : (j + 1) * TOK], low)
        inv = 1.0 / total
        rinv[h] = jnp.broadcast_to(inv, (8, TOK))
        att[h] = (out * inv).astype(jnp.bfloat16)

    def far_copy(kind, to):
        return remote(dfar.at[kind], rfar.at[kind], ds_s.at[0, kind], ds_r.at[0, kind], seq=to)

    def near_copy(kind, to):
        return remote(dnear.at[kind], rnear.at[kind], ds_s.at[1, kind], ds_r.at[1, kind], seq=to)

    def far_start(kind):
        dfar[kind] = dkv[kind, 0:TOK, :].astype(jnp.bfloat16)

        @pl.when(s >= 2)
        def _():
            far_copy(kind, s - 1).start()

        @pl.when((s == 0) | (s == 3))
        def _():
            rfar[kind] = jnp.zeros((TOK, HEAD), jnp.bfloat16)

    def near_start(kind):
        @pl.when(inner)
        def _():
            far_copy(kind, s + 1).wait_recv()

        both = dkv[kind, TOK : 2 * TOK, :] + rfar[kind].astype(jnp.float32)
        dnear[kind] = both.astype(jnp.bfloat16)

        @pl.when(s >= 1)
        def _():
            near_copy(kind, s - 1).start()

        @pl.when(s == 3)
        def _():
            rnear[kind] = jnp.zeros((TOK, HEAD), jnp.bfloat16)

    def first(k):
        to = lax.rem(y + 1 + k, 4)
        return remote(pacc.at[:, to], r1.at[k], s1.at[k], t1.at[k], dp=to * 2 + core)

    second = remote(p1.at[1 - core], r2, s2, t2, dp=partner)

    def third(k):
        part = p2.at[:, pl.ds((1 + k) * 128, 128)]
        return remote(part, r3.at[k], s3.at[k], t3.at[k], seq=lax.rem(s + 1 + k, 4))

    def after_first():
        mine = pacc[:, y]
        for k in range(3):
            first(k).wait_recv()
            mine = mine + r1[k]
        p1[...] = mine
        second.start()

    def after_second():
        second.wait_recv()
        p2[...] = p1[core] + r2[...]
        for k in range(3):
            third(k).start()

    def weight_block(h, d):
        return jnp.concatenate([wbuf[h, d % 2, d // 2, b] for b in range(4)], axis=1)

    def kv_all(k):
        return jnp.concatenate([kv[j, k] for j in range(BLOCKS)], axis=0)

    def group_sums(heads):
        att_h = jnp.concatenate([att[h] for h in heads], axis=0)
        for d in range(8):
            gw = mm(att_h, cot[:, d * 512 : (d + 1) * 512])
            for n, h in enumerate(heads):
                w = weight_block(h, d).astype(jnp.float32)
                pacc[d % 2, d // 2, pl.ds(h, 1), :] = jnp.sum(
                    gw[n * HEAD : (n + 1) * HEAD] * w, axis=0, keepdims=True
                )

    def grad_out(heads):
        go = jnp.zeros((len(heads) * HEAD, TOK), jnp.float32)
        for d in range(8):
            w = jnp.concatenate([weight_block(h, d) for h in heads], axis=0)
            go = go + mm(w, cot_t[d * 512 : (d + 1) * 512, :])
        for n, h in enumerate(heads):
            gout[h] = go[n * HEAD : (n + 1) * HEAD] * rinv[h, 0:1, :]

    def attention(h, last=False):
        go = gout[h]
        delta = jnp.sum(go * att[h].astype(jnp.float32), axis=0, keepdims=True)
        e = ebuf[h]
        dkv[1] += mm(e, jnp.transpose(go).astype(jnp.bfloat16))
        if last:
            far_start(1)
        dprob = mm(kv_all(1), go.astype(jnp.bfloat16))
        ds = (e.astype(jnp.float32) * (dprob - delta)).astype(jnp.bfloat16)
        dkv[0] += mm(ds, qh[h])
        if last:
            far_start(0)
            after_first()
        dq = mm(kv_t[0], ds)
        q_f32[pl.ds(h, TOK, stride=HEADS), :] = jnp.transpose(dq * SCALE)

    def y_start(c):
        z_arrive(way_a(c))
        ycopy(c, 0).start()
        ycopy(c, 1).start()
        pcopy(c, 0).start()

    y_start(0)

    def step(i, _):
        @pl.when(i < WAYS)
        def _():
            @pl.when(i + 3 < WAYS)
            def _():
                z_start(way_a(i + 3))

            @pl.when(i + 4 == WAYS)
            def _():
                for k in range(2):
                    hcopy(k).wait_recv()
                z_start(way_b)

            @pl.when(i + 2 < WAYS)
            def _():
                z_pass(way_a(i + 2))

            @pl.when(i + 1 == WAYS)
            def _():
                z_pass(way_b)

            @pl.when(i + 1 < WAYS)
            def _():
                y_start(i + 1)

            @pl.when(i == 0)
            def _():
                kv_start()
                query_inputs()

            @pl.when(i == 1)
            def _():
                for k in range(2):
                    ocopy(WAYS, k).wait_recv()
                    hcopy(k).start()
                cot_inputs()

        @pl.when((i >= 1) & (i < WAYS + 1))
        def _():
            c = i - 1
            for k in range(2):
                ocopy(c, k).wait_recv()
                ycopy(c, k).wait_recv()
                fcopy(c, k).start()
                pcopy(c, 1 + k).start()

        @pl.when((i >= 2) & (i < WAYS + 2))
        def _():
            c = i - 2
            fcopy(c, 0).wait_recv()
            fcopy(c, 1).wait_recv()
            pcopy(c, 3).start()

        @pl.when(i == 2)
        def _():
            kv_arrive(0)
            kv_send(1)

        @pl.when(i == 3)
        def _():
            attention_inputs()

        @pl.when(i == WAYS)
        def _():
            z_arrive(way_b)
            wcopy().start()

        def forward_turn(h, _):
            forward(h)
            return 0

        first_forward = jnp.where(i == 3, 0, jnp.where(i == 4, 4, 7))
        forwards = jnp.where(i == 3, 4, jnp.where(i == 4, 3, jnp.where(i == 5, 1, 0)))
        lax.fori_loop(first_forward, first_forward + forwards, forward_turn, 0)

        def attention_turn(n, _):
            attention(jnp.where(i == 8, 5 + 2 * n, jnp.where(i == 7, 4, i - 4 + n)))
            return 0

        count = jnp.where(i < 4, 0, jnp.where((i == 6) | (i == 8), 2, 1))
        lax.fori_loop(0, count, attention_turn, 0)

        @pl.when((i >= 2) & (i < WAYS + 1))
        def _():
            for k in range(4):
                pcopy(i - 2, k).wait_recv()

        @pl.when(i == WAYS)
        def _():
            wcopy().wait_recv()

        @pl.when((i == 3) | (i == 5) | (i == WAYS))
        def _():
            heads = (jnp.where(i == WAYS, 5, i - 3), jnp.where(i == WAYS, 7, i - 2))
            group_sums(heads)
            grad_out(heads)

        @pl.when(i == 6)
        def _():
            group_sums((4,))
            grad_out((4,))

        return 0

    lax.fori_loop(0, HEADS + 1, step, 0)

    final = WAYS - 1
    for k in range(4):
        pcopy(final, k).wait_recv()
    group_sums((final,))
    for k in range(3):
        first(k).start()
    grad_out((final,))
    attention(final, last=True)
    near_start(1)
    after_second()
    near_start(0)
    dq_ref[...] = q_f32[...].reshape(TOK, HEADS, HEAD).astype(jnp.bfloat16)
    total = p2[:, 0:128]
    for k in range(3):
        third(k).wait_recv()
        total = total + r3[k]
    gs_ref[...] = total * STEP_SCALE / step_ref[...].astype(jnp.float32)

    def z_sent(copy):
        for to in range(4):
            @pl.when(near(to))
            def _():
                copy(0, to, lax.rem(s + 4 - to, 4), to).wait_send()

        @pl.when(inner)
        def _():
            copy(2, end, end_slot, 4).wait_send()

    def sent(c, _):
        z_sent(way_a(c))
        for k in range(2):
            ocopy(c, k).wait_send()
            ycopy(c, k).wait_send()
            fcopy(c, k).wait_send()
        for k in range(4):
            pcopy(c, k).wait_send()
        return 0

    lax.fori_loop(0, WAYS, sent, 0)
    z_sent(way_b)
    for k in range(2):
        ocopy(WAYS, k).wait_send()
        hcopy(k).wait_send()
    wcopy().wait_send()
    for k in range(2):
        @pl.when((s < 3) & (s >= k))
        def _():
            seg_copy(k).wait_send()
            kv_copy(k).wait_send()

    for k in range(3):
        first(k).wait_send()
        third(k).wait_send()
    second.wait_send()

    own = slice(2 * TOK, 3 * TOK)
    for kind, scale, out_ref in ((1, 1.0, dv_ref), (0, SCALE, dk_ref)):
        @pl.when(s < 3)
        def _():
            near_copy(kind, s + 1).wait_recv()

        total = dkv[kind, own, :] + rnear[kind].astype(jnp.float32)
        out_ref[...] = (total * scale).astype(jnp.bfloat16)

        @pl.when(s >= 2)
        def _():
            far_copy(kind, s - 1).wait_send()

        @pl.when(s >= 1)
        def _():
            near_copy(kind, s - 1).wait_send()


def hand_over(*refs):
    for k in range(4):
        refs[4 + k][...] = refs[k][...]


def local(queries, keys, values, segment_ids, codes, zero_points, step_sizes, cotangent):
    bf16, f32, i32 = jnp.bfloat16, jnp.float32, jnp.int32
    dma = pltpu.SemaphoreType.DMA
    vmem = pltpu.VMEM
    in_vmem = pl.BlockSpec(memory_space=pltpu.VMEM)
    anywhere = pl.BlockSpec(memory_space=pl.ANY)
    results = pl.pallas_call(
        kernel,
        out_shape=(
            jax.ShapeDtypeStruct((HEADS, 128), f32),
            jax.ShapeDtypeStruct((TOK, HEADS, HEAD), bf16),
            jax.ShapeDtypeStruct((TOK, HEAD), bf16),
            jax.ShapeDtypeStruct((TOK, HEAD), bf16),
        ),
        in_specs=[anywhere, in_vmem, in_vmem, in_vmem, anywhere, in_vmem, in_vmem, anywhere],
        out_specs=(in_vmem, in_vmem, in_vmem, in_vmem),
        scratch_shapes=[
            vmem((TOK, HEADS, HEAD), bf16),
            vmem((TOK * HEADS, HEAD), f32),
            vmem((128, HEADS * HEAD), i32),
            vmem((TOK, DOUT), bf16),
            vmem((DOUT, TOK), bf16),
            vmem((HEADS, 2, 4, 4, HEAD, 128), bf16),
            vmem((BLOCKS, 2, TOK, HEAD), bf16),
            vmem((2, HEAD, BLOCKS * TOK), bf16),
            vmem((BLOCKS, 8, TOK), i32),
            vmem((BLOCKS * TOK, TOK), f32),
            vmem((HEADS, TOK, HEAD), bf16),
            vmem((BLOCKS * TOK, TOK), f32),
            vmem((HEADS, BLOCKS * TOK, TOK), bf16),
            vmem((HEADS, HEAD, TOK), bf16),
            vmem((HEADS, 8, TOK), f32),
            vmem((HEADS, HEAD, TOK), f32),
            vmem((2, 4, HEADS, 512), f32),
            vmem((2, BLOCKS * TOK, HEAD), f32),
            vmem((2, HEADS, 512), f32),
            vmem((3, 2, HEADS, 512), f32),
            vmem((HEADS, 512), f32),
            vmem((HEADS, 512), f32),
            vmem((3, HEADS, 128), f32),
            vmem((2, TOK, HEAD), bf16),
            vmem((2, TOK, HEAD), bf16),
            vmem((2, TOK, HEAD), bf16),
            vmem((2, TOK, HEAD), bf16),
            dma((3,)),
            dma((HEADS, 5)), dma((HEADS, 4)),
            dma((HEADS, 2)), dma((HEADS, 2)), dma((HEADS, 2)), dma((HEADS, 2)), dma((HEADS, 2)), dma((HEADS, 2)),
            dma((HEADS, 4)), dma((HEADS, 4)),
            dma((2,)), dma((2,)), dma((2,)), dma((2,)),
            dma((3,)), dma((3,)), dma, dma, dma((3,)), dma((3,)),
            dma((2, 2)), dma((2, 2)),
        ],
        compiler_params=pltpu.CompilerParams(
            collective_id=0, has_side_effects=True, vmem_limit_bytes=56 * 2**20
        ),
        name="fused",
    )(
        queries[0], keys.reshape(TOK, HEAD), values.reshape(TOK, HEAD), segment_ids,
        codes, zero_points.T, step_sizes.T, cotangent[0],
    )
    steps, dq, dk, dv = pl.pallas_call(
        hand_over,
        out_shape=[jax.ShapeDtypeStruct(r.shape, r.dtype) for r in results],
        in_specs=[in_vmem] * 4,
        out_specs=[in_vmem] * 4,
        name="hand_over",
    )(*results)
    return (steps.T, dq[None], dk.reshape(1, TOK, 1, HEAD), dv.reshape(1, TOK, 1, HEAD))


def solution(mesh):
    in_specs = (
        P("dp", "seq", "tensor", None),
        P("dp", "seq", "tensor", None),
        P("dp", "seq", "tensor", None),
        P("dp", "seq"),
        P(("dp", "seq"), "tensor"),
        P(("dp", "seq"), "tensor"),
        P(("dp", "seq"), "tensor"),
        P("dp", "seq", None),
    )
    out_specs = (
        P(("dp", "seq"), "tensor"),
        P("dp", "seq", "tensor", None),
        P("dp", "seq", "tensor", None),
        P("dp", "seq", "tensor", None),
    )
    return jax.shard_map(local, mesh=mesh, in_specs=in_specs, out_specs=out_specs, check_vma=False)
```

```python
import jax
import jax.numpy as jnp
from jax import lax
from jax.experimental import pallas as pl
from jax.experimental.pallas import tpu as pltpu
from jax.sharding import PartitionSpec as P

MESH = pl.DeviceIdType.MESH
HEADS = 8
HEAD = 128
TOK = 256
DOUT = 4096
BLOCKS = 3
WAYS = 7
SCALE = HEAD**-0.5
LOG2E = 1.4426950408889634
STEP_SCALE = 8192**-0.5
NT = (((1,), (1,)), ((), ()))


def mm(a, b):
    return jnp.dot(a, b, preferred_element_type=jnp.float32)


def kernel(
    q_hbm, k_ref, v_ref, seg_ref, codes_hbm, zero_ref, step_ref, cot_hbm,
    gs_ref, dq_ref, dk_ref, dv_ref,
    q_in, q_f32, codes, cot, cot_t, wbuf, kv, kv_t, seg, bias, qh, xbuf, ebuf, att, rinv, gout, pacc, dkv,
    p1, r1, p2, r2, r3, dfar, dnear, rfar, rnear,
    in_sem, zs, zr, os, ors, ys, yr, fs, fr, ps, pr, kvs, kvr, sgs, sgr, s1, t1, s2, t2, s3, t3, ds_s, ds_r,
):
    dp = lax.axis_index("dp")
    s = lax.axis_index("seq")
    core = lax.rem(dp, 2)
    y = dp // 2
    partner = dp + 1 - 2 * core
    yp = lax.rem(y + 1, 4)
    ym = lax.rem(y + 3, 4)
    y2 = lax.rem(y + 2, 4)

    in_codes = pltpu.make_async_copy(codes_hbm, codes, in_sem.at[0])
    in_q = pltpu.make_async_copy(q_hbm, q_in, in_sem.at[1])
    in_cot = pltpu.make_async_copy(cot_hbm, cot, in_sem.at[2])
    in_codes.start()
    in_q.start()

    def cot_piece(d, slot):
        source = pl.multiple_of(d * 512 + lax.rem(slot + s, 4) * 128, 128)
        target = pl.multiple_of(d * 512 + slot * 128, 128)
        return pltpu.make_async_copy(
            cot_hbm.at[:, pl.ds(source, 128)], cot.at[:, pl.ds(target, 128)], in_sem.at[2]
        )

    def cot_start(d, _):
        for slot in range(4):
            cot_piece(d, slot).start()
        return 0


    barrier = pltpu.get_barrier_semaphore()
    for other in (partner, yp * 2 + core, ym * 2 + core, y2 * 2 + core):
        pl.semaphore_signal(barrier, inc=1, device_id={"dp": other}, device_id_type=MESH)
    for k in (1, 2, 3):
        pl.semaphore_signal(
            barrier, inc=1, device_id={"seq": lax.rem(s + k, 4)}, device_id_type=MESH
        )

    def remote(src, dst, send, recv, **to):
        return pltpu.make_async_remote_copy(
            src, dst, send, recv, device_id=to, device_id_type=MESH
        )

    def zcopy(c, slot, to, to_slot, send):
        return remote(
            wbuf.at[c, core, y, slot], wbuf.at[c, core, y, to_slot], send, zr.at[c, to_slot], seq=to
        )

    def bcopy(slot, to, to_slot, send):
        c = WAYS
        return remote(
            wbuf.at[c, core, :, slot], wbuf.at[c, core, :, to_slot], send, zr.at[c, to_slot], seq=to
        )

    def ycopy(c, k):
        part = wbuf.at[c, core, y, pl.ds(1, 3)]
        return remote(part, part, ys.at[c, k], yr.at[c, k], dp=(yp, ym)[k] * 2 + core)

    def ocopy(c, k):
        part = wbuf.at[c, core, y, 0]
        return remote(part, part, os.at[c, k], ors.at[c, k], dp=(yp, ym)[k] * 2 + core)

    def fcopy(c, k):
        part = wbuf.at[c, core, (ym, yp)[k], pl.ds(k * 2, 2)]
        return remote(part, part, fs.at[c, k], fr.at[c, k], dp=(yp, ym)[k] * 2 + core)

    def hcopy(k):
        part = wbuf.at[WAYS, core, (ym, yp)[k], 0, pl.ds(k * 64, 64)]
        return remote(part, part, fs.at[WAYS, k], fr.at[WAYS, k], dp=(yp, ym)[k] * 2 + core)

    def pcopy(c, k):
        part = wbuf.at[c, core, (y, ym, yp, y2)[k]]
        return remote(part, part, ps.at[c, k], pr.at[c, k], dp=partner)

    def wcopy():
        part = wbuf.at[WAYS, core]
        return remote(part, part, ps.at[WAYS, 0], pr.at[WAYS, 0], dp=partner)

    def near(to):
        return (jnp.abs(s - to) == 1) | (jnp.abs(s - to) == 2)

    inner = (s == 1) | (s == 2)
    end = jnp.where(s == 2, 3, 0)
    end_slot = jnp.where(s == 2, 1, 3)

    def own_start(c):
        for k in range(2):
            ocopy(c, k).start()

    def z_start(copy):
        for to in range(4):
            @pl.when(near(to))
            def _():
                copy(0, to, lax.rem(s + 4 - to, 4), to).start()

    def z_pass(copy):
        @pl.when(inner)
        def _():
            copy(0, s, 2, 0).wait_recv()
            copy(2, end, end_slot, 4).start()

    def z_arrive(copy):
        for slot in range(1, 4):
            def wait():
                copy(0, s, slot, 0).wait_recv()

            if slot == 2:
                pl.when(jnp.logical_not(inner))(wait)
            else:
                wait()

    def way_a(c):
        return lambda slot, to, to_slot, k: zcopy(c, slot, to, to_slot, zs.at[c, k])

    def way_b(slot, to, to_slot, k):
        return bcopy(slot, to, to_slot, zs.at[WAYS, k])

    def make_weight(h):
        part = jnp.transpose(codes[:, h * HEAD : (h + 1) * HEAD].astype(jnp.float32))
        zero = zero_ref[h : h + 1, :].astype(jnp.float32)
        step = step_ref[...].astype(jnp.float32)[h : h + 1, :]
        wbuf[h, core, y, 0] = ((part - zero) * step).astype(jnp.bfloat16)

    def kv_copy(k):
        return remote(kv.at[2 - k], kv.at[1 - k], kvs.at[k], kvr.at[k], seq=s + 1)

    def seg_copy(k):
        return remote(seg.at[2 - k], seg.at[1 - k], sgs.at[k], sgr.at[k], seq=s + 1)

    def kv_send(k):
        @pl.when((s < 3) & (s >= k))
        def _():
            seg_copy(k).start()
            kv_copy(k).start()

    def kv_arrive(k):
        @pl.when(s >= 1 + k)
        def _():
            remote(kv.at[2 - k], kv.at[1 - k], kvs.at[k], kvr.at[k], seq=s - 1).wait_recv()
            remote(seg.at[2 - k], seg.at[1 - k], sgs.at[k], sgr.at[k], seq=s - 1).wait_recv()

    in_codes.wait()
    make_weight(0)
    pl.semaphore_wait(barrier, 7)
    z_start(way_a(0))
    own_start(0)
    make_weight(1)
    z_start(way_a(1))
    own_start(1)
    make_weight(2)
    z_start(way_a(2))
    own_start(2)
    for h in (WAYS, *range(3, WAYS)):
        make_weight(h)
        own_start(h)
    lax.fori_loop(0, 8, cot_start, 0)
    z_pass(way_a(0))
    z_pass(way_a(1))

    def kv_start():
        kv[2, 0] = k_ref[...]
        kv[2, 1] = v_ref[...]
        seg[2] = jnp.broadcast_to(seg_ref[...], (8, TOK))
        for k in range(2):
            @pl.when(s - 1 - k < 0)
            def _():
                kv[1 - k] = jnp.zeros((2, TOK, HEAD), jnp.bfloat16)
                seg[1 - k] = jnp.full((8, TOK), -1, jnp.int32)

        kv_send(0)

    def query_inputs():
        in_q.wait()
        q_f32[...] = q_in[...].astype(jnp.float32).reshape(TOK * HEADS, HEAD)
        for h in range(HEADS):
            qh[h] = q_f32[pl.ds(h, TOK, stride=HEADS), :].astype(jnp.bfloat16)
        dkv[...] = jnp.zeros((2, BLOCKS * TOK, HEAD), jnp.float32)

    def cot_inputs():
        in_cot.wait()

        def turn(i, _):
            part = cot[:, pl.ds(pl.multiple_of(i * 512, 512), 512)].astype(jnp.float32)
            cot_t[pl.ds(pl.multiple_of(i * 512, 512), 512), :] = jnp.transpose(part).astype(
                jnp.bfloat16
            )
            return 0

        lax.fori_loop(0, 8, turn, 0)

    def attention_inputs():
        kv_arrive(1)
        own = seg_ref[...].astype(jnp.float32)
        for j in range(BLOCKS):
            kv_t[0, :, j * TOK : (j + 1) * TOK] = jnp.transpose(
                kv[j, 0].astype(jnp.float32)
            ).astype(jnp.bfloat16)
            kv_t[1, :, j * TOK : (j + 1) * TOK] = jnp.transpose(
                kv[j, 1].astype(jnp.float32)
            ).astype(jnp.bfloat16)
            for half in range(2):
                row = seg[j, 0:1, half * 128 : (half + 1) * 128].astype(jnp.float32)
                column = jnp.transpose(jnp.broadcast_to(row, (128, 128)))
                column = jnp.concatenate([column, column], axis=1)
                allowed = column == own
                if j == BLOCKS - 1:
                    key_pos = half * 128 + lax.broadcasted_iota(jnp.int32, (128, TOK), 0)
                    query_pos = lax.broadcasted_iota(jnp.int32, (128, TOK), 1)
                    allowed = allowed & (key_pos <= query_pos)
                bias[j * TOK + half * 128 : j * TOK + (half + 1) * 128, :] = jnp.where(
                    allowed, jnp.float32(0.0), jnp.float32(-1e30)
                )

    def forward(h):
        q = qh[h]
        top = jnp.full((1, TOK), -1e30, jnp.float32)
        for j in range(BLOCKS):
            x = lax.dot_general(kv[j, 0], q, NT, preferred_element_type=jnp.float32)
            x = x * (SCALE * LOG2E) + bias[j * TOK : (j + 1) * TOK, :]
            xbuf[j * TOK : (j + 1) * TOK, :] = x
            top = jnp.maximum(top, jnp.max(x, axis=0, keepdims=True))
        total = jnp.zeros((1, TOK), jnp.float32)
        out = jnp.zeros((HEAD, TOK), jnp.float32)
        for j in range(BLOCKS):
            e = jnp.exp2(xbuf[j * TOK : (j + 1) * TOK, :] - top)
            total = total + jnp.sum(e, axis=0, keepdims=True)
            low = e.astype(jnp.bfloat16)
            ebuf[h, j * TOK : (j + 1) * TOK, :] = low
            out = out + mm(kv_t[1, :, j * TOK : (j + 1) * TOK], low)
        inv = 1.0 / total
        rinv[h] = jnp.broadcast_to(inv, (8, TOK))
        att[h] = (out * inv).astype(jnp.bfloat16)

    def far_copy(kind, to):
        return remote(dfar.at[kind], rfar.at[kind], ds_s.at[0, kind], ds_r.at[0, kind], seq=to)

    def near_copy(kind, to):
        return remote(dnear.at[kind], rnear.at[kind], ds_s.at[1, kind], ds_r.at[1, kind], seq=to)

    def far_start(kind):
        dfar[kind] = dkv[kind, 0:TOK, :].astype(jnp.bfloat16)

        @pl.when(s >= 2)
        def _():
            far_copy(kind, s - 1).start()

        @pl.when((s == 0) | (s == 3))
        def _():
            rfar[kind] = jnp.zeros((TOK, HEAD), jnp.bfloat16)

    def near_start(kind):
        @pl.when(inner)
        def _():
            far_copy(kind, s + 1).wait_recv()

        both = dkv[kind, TOK : 2 * TOK, :] + rfar[kind].astype(jnp.float32)
        dnear[kind] = both.astype(jnp.bfloat16)

        @pl.when(s >= 1)
        def _():
            near_copy(kind, s - 1).start()

        @pl.when(s == 3)
        def _():
            rnear[kind] = jnp.zeros((TOK, HEAD), jnp.bfloat16)

    def first(k):
        to = lax.rem(y + 1 + k, 4)
        return remote(pacc.at[:, to], r1.at[k], s1.at[k], t1.at[k], dp=to * 2 + core)

    second = remote(p1.at[1 - core], r2, s2, t2, dp=partner)

    def third(k):
        part = p2.at[:, pl.ds((1 + k) * 128, 128)]
        return remote(part, r3.at[k], s3.at[k], t3.at[k], seq=lax.rem(s + 1 + k, 4))

    def after_first():
        mine = pacc[:, y]
        for k in range(3):
            first(k).wait_recv()
            mine = mine + r1[k]
        p1[...] = mine
        second.start()

    def after_second():
        second.wait_recv()
        p2[...] = p1[core] + r2[...]
        for k in range(3):
            third(k).start()

    def weight_block(h, d):
        return jnp.concatenate([wbuf[h, d % 2, d // 2, b] for b in range(4)], axis=1)

    def kv_all(k):
        return jnp.concatenate([kv[j, k] for j in range(BLOCKS)], axis=0)

    def group_sums(heads):
        att_h = jnp.concatenate([att[h] for h in heads], axis=0)
        for d in range(8):
            gw = mm(att_h, cot[:, d * 512 : (d + 1) * 512])
            for n, h in enumerate(heads):
                w = weight_block(h, d).astype(jnp.float32)
                pacc[d % 2, d // 2, pl.ds(h, 1), :] = jnp.sum(
                    gw[n * HEAD : (n + 1) * HEAD] * w, axis=0, keepdims=True
                )

    def grad_out(heads):
        go = jnp.zeros((len(heads) * HEAD, TOK), jnp.float32)
        for d in range(8):
            w = jnp.concatenate([weight_block(h, d) for h in heads], axis=0)
            go = go + mm(w, cot_t[d * 512 : (d + 1) * 512, :])
        for n, h in enumerate(heads):
            gout[h] = go[n * HEAD : (n + 1) * HEAD] * rinv[h, 0:1, :]

    def attention(h, last=False):
        go = gout[h]
        delta = jnp.sum(go * att[h].astype(jnp.float32), axis=0, keepdims=True)
        e = ebuf[h]
        dkv[1] += mm(e, jnp.transpose(go).astype(jnp.bfloat16))
        if last:
            far_start(1)
        dprob = mm(kv_all(1), go.astype(jnp.bfloat16))
        ds = (e.astype(jnp.float32) * (dprob - delta)).astype(jnp.bfloat16)
        dkv[0] += mm(ds, qh[h])
        if last:
            far_start(0)
            after_first()
        dq = mm(kv_t[0], ds)
        q_f32[pl.ds(h, TOK, stride=HEADS), :] = jnp.transpose(dq * SCALE)

    def y_start(c):
        z_arrive(way_a(c))
        ycopy(c, 0).start()
        ycopy(c, 1).start()
        pcopy(c, 0).start()

    y_start(0)

    def step(i, _):
        @pl.when(i < WAYS)
        def _():
            @pl.when(i + 3 < WAYS)
            def _():
                z_start(way_a(i + 3))

            @pl.when(i + 3 == WAYS)
            def _():
                for k in range(2):
                    hcopy(k).wait_recv()
                z_start(way_b)

            @pl.when(i + 2 < WAYS)
            def _():
                z_pass(way_a(i + 2))

            @pl.when(i + 1 == WAYS)
            def _():
                z_pass(way_b)

            @pl.when(i + 1 < WAYS)
            def _():
                y_start(i + 1)

            @pl.when(i == 0)
            def _():
                kv_start()
                query_inputs()

            @pl.when(i == 1)
            def _():
                for k in range(2):
                    ocopy(WAYS, k).wait_recv()
                    hcopy(k).start()
                cot_inputs()

        @pl.when((i >= 1) & (i < WAYS + 1))
        def _():
            c = i - 1
            for k in range(2):
                ocopy(c, k).wait_recv()
                ycopy(c, k).wait_recv()
                fcopy(c, k).start()
                pcopy(c, 1 + k).start()

        @pl.when((i >= 2) & (i < WAYS + 2))
        def _():
            c = i - 2
            fcopy(c, 0).wait_recv()
            fcopy(c, 1).wait_recv()
            pcopy(c, 3).start()

        @pl.when(i == 2)
        def _():
            kv_arrive(0)
            kv_send(1)

        @pl.when(i == 3)
        def _():
            attention_inputs()

        @pl.when(i == WAYS)
        def _():
            z_arrive(way_b)
            wcopy().start()

        def forward_turn(h, _):
            forward(h)
            return 0

        first_forward = jnp.where(i == 3, 0, jnp.where(i == 4, 4, 7))
        forwards = jnp.where(i == 3, 4, jnp.where(i == 4, 3, jnp.where(i == 5, 1, 0)))
        lax.fori_loop(first_forward, first_forward + forwards, forward_turn, 0)

        def attention_turn(n, _):
            attention(jnp.where(i == 8, 5 + 2 * n, jnp.where(i == 7, 4, i - 4 + n)))
            return 0

        count = jnp.where(i < 4, 0, jnp.where((i == 6) | (i == 8), 2, 1))
        lax.fori_loop(0, count, attention_turn, 0)

        @pl.when((i >= 2) & (i < WAYS + 1))
        def _():
            for k in range(4):
                pcopy(i - 2, k).wait_recv()

        @pl.when(i == WAYS)
        def _():
            wcopy().wait_recv()

        @pl.when((i == 3) | (i == 5) | (i == WAYS))
        def _():
            heads = (jnp.where(i == WAYS, 5, i - 3), jnp.where(i == WAYS, 7, i - 2))
            group_sums(heads)
            grad_out(heads)

        @pl.when(i == 6)
        def _():
            group_sums((4,))
            grad_out((4,))

        return 0

    lax.fori_loop(0, HEADS + 1, step, 0)

    final = WAYS - 1
    for k in range(4):
        pcopy(final, k).wait_recv()
    group_sums((final,))
    for k in range(3):
        first(k).start()
    grad_out((final,))
    attention(final, last=True)
    near_start(1)
    after_second()
    near_start(0)
    dq_ref[...] = q_f32[...].reshape(TOK, HEADS, HEAD).astype(jnp.bfloat16)
    total = p2[:, 0:128]
    for k in range(3):
        third(k).wait_recv()
        total = total + r3[k]
    gs_ref[...] = total * STEP_SCALE / step_ref[...].astype(jnp.float32)

    def z_sent(copy):
        for to in range(4):
            @pl.when(near(to))
            def _():
                copy(0, to, lax.rem(s + 4 - to, 4), to).wait_send()

        @pl.when(inner)
        def _():
            copy(2, end, end_slot, 4).wait_send()

    def sent(c, _):
        z_sent(way_a(c))
        for k in range(2):
            ocopy(c, k).wait_send()
            ycopy(c, k).wait_send()
            fcopy(c, k).wait_send()
        for k in range(4):
            pcopy(c, k).wait_send()
        return 0

    lax.fori_loop(0, WAYS, sent, 0)
    z_sent(way_b)
    for k in range(2):
        ocopy(WAYS, k).wait_send()
        hcopy(k).wait_send()
    wcopy().wait_send()
    for k in range(2):
        @pl.when((s < 3) & (s >= k))
        def _():
            seg_copy(k).wait_send()
            kv_copy(k).wait_send()

    for k in range(3):
        first(k).wait_send()
        third(k).wait_send()
    second.wait_send()

    own = slice(2 * TOK, 3 * TOK)
    for kind, scale, out_ref in ((1, 1.0, dv_ref), (0, SCALE, dk_ref)):
        @pl.when(s < 3)
        def _():
            near_copy(kind, s + 1).wait_recv()

        total = dkv[kind, own, :] + rnear[kind].astype(jnp.float32)
        out_ref[...] = (total * scale).astype(jnp.bfloat16)

        @pl.when(s >= 2)
        def _():
            far_copy(kind, s - 1).wait_send()

        @pl.when(s >= 1)
        def _():
            near_copy(kind, s - 1).wait_send()


def hand_over(*refs):
    for k in range(4):
        refs[4 + k][...] = refs[k][...]


def local(queries, keys, values, segment_ids, codes, zero_points, step_sizes, cotangent):
    bf16, f32, i32 = jnp.bfloat16, jnp.float32, jnp.int32
    dma = pltpu.SemaphoreType.DMA
    vmem = pltpu.VMEM
    in_vmem = pl.BlockSpec(memory_space=pltpu.VMEM)
    anywhere = pl.BlockSpec(memory_space=pl.ANY)
    results = pl.pallas_call(
        kernel,
        out_shape=(
            jax.ShapeDtypeStruct((HEADS, 128), f32),
            jax.ShapeDtypeStruct((TOK, HEADS, HEAD), bf16),
            jax.ShapeDtypeStruct((TOK, HEAD), bf16),
            jax.ShapeDtypeStruct((TOK, HEAD), bf16),
        ),
        in_specs=[anywhere, in_vmem, in_vmem, in_vmem, anywhere, in_vmem, in_vmem, anywhere],
        out_specs=(in_vmem, in_vmem, in_vmem, in_vmem),
        scratch_shapes=[
            vmem((TOK, HEADS, HEAD), bf16),
            vmem((TOK * HEADS, HEAD), f32),
            vmem((128, HEADS * HEAD), i32),
            vmem((TOK, DOUT), bf16),
            vmem((DOUT, TOK), bf16),
            vmem((HEADS, 2, 4, 4, HEAD, 128), bf16),
            vmem((BLOCKS, 2, TOK, HEAD), bf16),
            vmem((2, HEAD, BLOCKS * TOK), bf16),
            vmem((BLOCKS, 8, TOK), i32),
            vmem((BLOCKS * TOK, TOK), f32),
            vmem((HEADS, TOK, HEAD), bf16),
            vmem((BLOCKS * TOK, TOK), f32),
            vmem((HEADS, BLOCKS * TOK, TOK), bf16),
            vmem((HEADS, HEAD, TOK), bf16),
            vmem((HEADS, 8, TOK), f32),
            vmem((HEADS, HEAD, TOK), f32),
            vmem((2, 4, HEADS, 512), f32),
            vmem((2, BLOCKS * TOK, HEAD), f32),
            vmem((2, HEADS, 512), f32),
            vmem((3, 2, HEADS, 512), f32),
            vmem((HEADS, 512), f32),
            vmem((HEADS, 512), f32),
            vmem((3, HEADS, 128), f32),
            vmem((2, TOK, HEAD), bf16),
            vmem((2, TOK, HEAD), bf16),
            vmem((2, TOK, HEAD), bf16),
            vmem((2, TOK, HEAD), bf16),
            dma((3,)),
            dma((HEADS, 5)), dma((HEADS, 4)),
            dma((HEADS, 2)), dma((HEADS, 2)), dma((HEADS, 2)), dma((HEADS, 2)), dma((HEADS, 2)), dma((HEADS, 2)),
            dma((HEADS, 4)), dma((HEADS, 4)),
            dma((2,)), dma((2,)), dma((2,)), dma((2,)),
            dma((3,)), dma((3,)), dma, dma, dma((3,)), dma((3,)),
            dma((2, 2)), dma((2, 2)),
        ],
        compiler_params=pltpu.CompilerParams(
            collective_id=0, has_side_effects=True, vmem_limit_bytes=56 * 2**20
        ),
        name="fused",
    )(
        queries[0], keys.reshape(TOK, HEAD), values.reshape(TOK, HEAD), segment_ids,
        codes, zero_points.T, step_sizes.T, cotangent[0],
    )
    steps, dq, dk, dv = pl.pallas_call(
        hand_over,
        out_shape=[jax.ShapeDtypeStruct(r.shape, r.dtype) for r in results],
        in_specs=[in_vmem] * 4,
        out_specs=[in_vmem] * 4,
        name="hand_over",
    )(*results)
    return (steps.T, dq[None], dk.reshape(1, TOK, 1, HEAD), dv.reshape(1, TOK, 1, HEAD))


def solution(mesh):
    in_specs = (
        P("dp", "seq", "tensor", None),
        P("dp", "seq", "tensor", None),
        P("dp", "seq", "tensor", None),
        P("dp", "seq"),
        P(("dp", "seq"), "tensor"),
        P(("dp", "seq"), "tensor"),
        P(("dp", "seq"), "tensor"),
        P("dp", "seq", None),
    )
    out_specs = (
        P(("dp", "seq"), "tensor"),
        P("dp", "seq", "tensor", None),
        P("dp", "seq", "tensor", None),
        P("dp", "seq", "tensor", None),
    )
    return jax.shard_map(local, mesh=mesh, in_specs=in_specs, out_specs=out_specs, check_vma=False)
```
